32 devices in a mesh: parts: 2 (over y), docs: 4 (over z), heads: 2 (over x), sub: 2 (over core).
Axes of the slice: x: 2, y: 2, z: 4, core: 2. Of those that a mesh axis runs over, the one named last changes fastest.
Arguments:
- hidden_rows: bfloat16 [16, 128, 8192], P(('parts', 'docs'), None, ('heads', 'sub')), parts along dimension 0, may hold values from -4200 to 4200
- norm_gain: bfloat16 [8192], P(('heads', 'sub')), may hold values from 0.099609375 to 1.8984375
- key_weight: bfloat16 [8192, 512], P(('heads', 'sub')), may hold values from -0.0625 to 0.0625
- value_weight: bfloat16 [8192, 512], P(('heads', 'sub')), may hold values from -0.0625 to 0.0625
- recompute_block: int32 [16], P(('parts', 'docs')), parts along dimension 0, may hold values from 0 to 3
- cache_keys: bfloat16 [16, 512, 512], P(('parts', 'docs'), 'sub', 'heads'), parts along dimension 0, may hold values from -6 to 6
- cache_values: bfloat16 [16, 512, 512], P(('parts', 'docs'), 'sub', 'heads'), parts along dimension 0, may hold values from -6 to 6
- slot_of_doc: int32 [16], P('parts'), parts along dimension 0, may hold values from 0 to 7, as said below
- session_docs: int32 [8, 3], P('parts'), parts along dimension 0, may hold values from -1 to 7, as said below
- session_count: int32 [8], P('parts'), parts along dimension 0, may hold values from 1 to 3, as said below
- turn_queries: bfloat16 [8, 128, 4096], P(('parts', 'docs'), None, 'heads'), parts along dimension 0, may hold values from -170 to 170
- turn_keys: bfloat16 [8, 128, 512], P(('parts', 'docs'), 'sub', 'heads'), parts along dimension 0, may hold values from -6 to 6
- turn_values: bfloat16 [8, 128, 512], P(('parts', 'docs'), 'sub', 'heads'), parts along dimension 0, may hold values from -6 to 6
- turn_length: int32 [8], P(('parts', 'docs')), parts along dimension 0, may hold values from 32 to 128, as said below
Outputs:
- attended: bfloat16 [8, 128, 4096], P(('parts', 'docs'), 'sub', 'heads'), parts along dimension 0
The draws below stay inside these ranges and needn't reach their ends.
There are 2 independent parts, one for each index of `parts`. The reference program is written for one: setup_inputs(seed, part) draws one part's arguments, and reference() takes and returns one part's arrays. A program takes and returns all parts, laid end to end along the dimension named above; an argument that names none is the same for every part. Nothing has to cross between parts.
Inputs may be any that keep to these rules, and one draw needn't show every extreme that they name: `session_docs`: row e lists session e's documents in its first session_count[e] entries and -1 after them; one session's documents are distinct and their slots slot_of_doc[doc] lie on distinct indices of docs (slot // 2). `session_count`: some session has exactly 3 documents and some exactly 1. `slot_of_doc`: a permutation; a document's cache rows, hidden rows and block index stand at its slot. `turn_length`: some session has exactly 128 tokens and some exactly 32.
All inputs are finite; a program needn't handle non-finite values.
Results may differ from the reference program's by a relative error of at most 0.012.
Values may be sent and summed in bfloat16 or wider, within the bound.
A program may use at most 64 MiB of HBM per device.

```python
import math
import jax
import jax.numpy as jnp
from jax import lax

D = 8192
HD = 128
KVH = 4
QH = 32
BLK = 128
DOCLEN = 512
DOC_DEV = 2
QLEN = 128
GQA = 8
NBLK = 4
NDOC = 8
SESSIONS = 4
DOCS_MIN = 1
DOCS_MAX = 3
QMIN = 32
N_DOCS = 4


def session_plan(key):
    key_count, key_owner, key_local, key_place, key_shuffle = jax.random.split(key, 5)
    counts = jax.random.randint(key_count, (SESSIONS,), DOCS_MIN, DOCS_MAX + 1)
    shuffled = jax.random.permutation(key_shuffle, SESSIONS)
    counts = counts.at[shuffled[0]].set(DOCS_MAX).at[shuffled[1]].set(DOCS_MIN)
    owner_keys = jax.random.split(key_owner, SESSIONS)
    owners = jax.vmap(lambda one_key: jax.random.permutation(one_key, N_DOCS))(owner_keys)[:, :DOCS_MAX]
    local_index = jax.random.randint(key_local, (SESSIONS, DOCS_MAX), 0, DOC_DEV)
    slots = owners * DOC_DEV + local_index
    placement = jax.random.permutation(key_place, NDOC)
    doc_at_slot = jnp.argsort(placement)
    doc_ids = doc_at_slot[slots]
    in_list = jnp.arange(DOCS_MAX)[None, :] < counts[:, None]
    doc_ids = jnp.where(in_list, doc_ids, -1)
    return (doc_ids.astype(jnp.int32), counts.astype(jnp.int32), placement.astype(jnp.int32))


def draw_session_docs(key, part):
    doc_ids, counts, placement = session_plan(key)
    return doc_ids


def draw_session_count(key, part):
    doc_ids, counts, placement = session_plan(key)
    return counts


def draw_slot_of_doc(key, part):
    doc_ids, counts, placement = session_plan(key)
    return placement


def turn_base(key):
    key_mean, key_noise = jax.random.split(key, 2)
    centre = 0.7 * jnp.clip(jax.random.normal(key_mean, (SESSIONS, 1, KVH * HD)), -4.0, 4.0)
    noise = jnp.clip(jax.random.normal(key_noise, (SESSIONS, QLEN, KVH * HD)), -4.0, 4.0)
    return centre + 0.7 * noise


def draw_turn_keys(key, part):
    rows_out = turn_base(key)
    return rows_out.astype(jnp.bfloat16)


def draw_turn_queries(key, part):
    key = jax.random.fold_in(key, 11)
    rows_out = 1.5 * jnp.clip(jax.random.normal(key, (SESSIONS, QLEN, QH * HD)), -4.0, 4.0)
    return rows_out.astype(jnp.bfloat16)


def cache_rows(key, centre_scale, noise_scale):
    key_mean, key_noise = jax.random.split(key, 2)
    centre = jnp.clip(jax.random.normal(key_mean, (NDOC, 1, KVH * HD)), -4.0, 4.0)
    noise = jnp.clip(jax.random.normal(key_noise, (NDOC, DOCLEN, KVH * HD)), -4.0, 4.0)
    return (centre_scale * centre + noise_scale * noise).astype(jnp.bfloat16)


def draw_cache_keys(key, part):
    key = jax.random.fold_in(key, 5)
    return cache_rows(key, 0.7, 0.7)


def draw_cache_values(key, part):
    key = jax.random.fold_in(key, 7)
    return cache_rows(key, 0.8, 0.6)


def feature_ramp(top_factor):
    fraction = jnp.arange(D, dtype=jnp.float32) / (D - 1)
    return jnp.exp(fraction * math.log(top_factor)).reshape(1, 1, D)


def draw_hidden_rows(key, part):
    key = jax.random.fold_in(key, 13)
    key_rows, key_cols, key_body = jax.random.split(key, 3)
    row_scales = jnp.exp(jax.random.uniform(key_rows, (NDOC, BLK, 1), minval=0.0, maxval=math.log(10.0)))
    col_scales = jnp.exp(jax.random.uniform(key_cols, (1, 1, D), minval=0.0, maxval=math.log(10.0)))
    values = jnp.clip(jax.random.normal(key_body, (NDOC, BLK, D)), -4.0, 4.0)
    ramp = feature_ramp(4.0)
    return (values * row_scales * col_scales * ramp).astype(jnp.bfloat16)


def draw_turn_length(key, part):
    key = jax.random.fold_in(key, 17)
    key_length, key_shuffle = jax.random.split(key)
    lengths = jax.random.randint(key_length, (SESSIONS,), QMIN, QLEN + 1)
    shuffled = jax.random.permutation(key_shuffle, SESSIONS)
    lengths = lengths.at[shuffled[0]].set(QLEN).at[shuffled[1]].set(QMIN)
    return lengths.astype(jnp.int32)


def plant(values, stream_key, low, high):
    longest = values.shape.index(max(values.shape))
    spots = []
    for shift in (0, 1):
        where = [jax.random.randint(jax.random.fold_in(stream_key, axis), (), 0, length) for axis, length in enumerate(values.shape)]
        where[longest] = (where[longest] + shift) % values.shape[longest]
        spots.append(tuple(where))
    return values.at[spots[0]].set(low).at[spots[1]].set(high)


def level_of(rng, shape, shards, least, high):
    loudness, own = 1.0, jax.random.fold_in(rng, 6)
    for position, shards_of in shards:
        draws = jnp.exp(jax.random.uniform(jax.random.fold_in(own, position), (shards_of,), jnp.float32, least / len(shards), high / len(shards)))
        loudness = loudness * jnp.repeat(draws, shape[position] // shards_of).reshape([-1 if axis == position else 1 for axis in range(len(shape))])
    return loudness


def centred(rng, extent, deviation, most, cuts=(), kind=jnp.bfloat16):
    values = jax.random.normal(rng, extent, jnp.float32) * deviation
    if len(cuts) > 0:
        values = level_of(rng, extent, cuts, -0.22, 0.18) * values
    return jnp.clip(values, min=-most, max=most).astype(kind)


def setup_inputs(seed: int = 0, part: int = 0) -> dict:
    arg_keys = jax.random.split(jax.random.key(seed), 15)
    part_splits = jax.random.split(jax.random.fold_in(arg_keys[14], part), 15)
    return {
        "hidden_rows": draw_hidden_rows(jax.random.fold_in(jax.random.fold_in(arg_keys[14], part), 71), part),
        "norm_gain": jnp.clip(1.0 + 0.18 * jax.random.normal(arg_keys[1], (D,), jnp.float32), 0.099609375, 1.8984375).astype(jnp.bfloat16),
        "key_weight": centred(arg_keys[2], (D, KVH * HD), D ** -0.5, 0.0625, ((0, 4),)),
        "value_weight": centred(arg_keys[3], (D, KVH * HD), D ** -0.5, 0.0625, ((0, 4),)),
        "recompute_block": plant(jax.random.randint(part_splits[4], (NDOC,), 0, NBLK), jax.random.fold_in(part_splits[4], 1), 0, NBLK - 1).astype(jnp.int32),
        "cache_keys": draw_cache_keys(jax.random.fold_in(jax.random.fold_in(arg_keys[14], part), 71), part),
        "cache_values": draw_cache_values(jax.random.fold_in(jax.random.fold_in(arg_keys[14], part), 71), part),
        "slot_of_doc": draw_slot_of_doc(jax.random.fold_in(jax.random.fold_in(arg_keys[14], part), 71), part),
        "session_docs": draw_session_docs(jax.random.fold_in(jax.random.fold_in(arg_keys[14], part), 71), part),
        "session_count": draw_session_count(jax.random.fold_in(jax.random.fold_in(arg_keys[14], part), 71), part),
        "turn_queries": draw_turn_queries(jax.random.fold_in(jax.random.fold_in(arg_keys[14], part), 71), part),
        "turn_keys": draw_turn_keys(jax.random.fold_in(jax.random.fold_in(arg_keys[14], part), 71), part),
        "turn_values": centred(part_splits[12], (SESSIONS, QLEN, KVH * HD), 1.0, 6.0, ((0, 4), (1, 2), (2, 2))),
        "turn_length": draw_turn_length(jax.random.fold_in(jax.random.fold_in(arg_keys[14], part), 71), part),
    }


EPSILON = 1e-05
ROPE_BASE = 500000.0
NEGATIVE = -1e+30

def rotate(values, positions):
    half_dim = values.shape[-1] // 2
    exponent = jnp.arange(half_dim, dtype=jnp.float32) * (2.0 / values.shape[-1])
    frequency = ROPE_BASE ** (-exponent)
    angles = positions.astype(jnp.float32)[..., None, None] * frequency
    cos_part = jnp.cos(angles)
    sin_part = jnp.sin(angles)
    first_half = values[..., :half_dim]
    second_half = values[..., half_dim:]
    return jnp.concatenate([first_half * cos_part - second_half * sin_part, second_half * cos_part + first_half * sin_part], axis=-1)

def recompute(hidden_rows, norm_gain, key_weight, value_weight, recompute_block):
    squares = lax.optimization_barrier(jnp.sum(jnp.square(hidden_rows.astype(jnp.float32)), axis=-1))
    row_scale = lax.rsqrt(squares / D + EPSILON)
    scaled = (hidden_rows.astype(jnp.float32) * norm_gain.astype(jnp.float32)).astype(jnp.bfloat16)
    flat_rows = scaled.reshape(NDOC * BLK, D)
    key_proj = jnp.dot(flat_rows, key_weight, preferred_element_type=jnp.float32).reshape(NDOC, BLK, KVH, HD)
    value_proj = jnp.dot(flat_rows, value_weight, preferred_element_type=jnp.float32).reshape(NDOC, BLK, KVH, HD)
    key_proj = key_proj * row_scale[:, :, None, None]
    value_proj = value_proj * row_scale[:, :, None, None]
    positions = recompute_block[:, None] * BLK + jnp.arange(BLK, dtype=jnp.int32)[None, :]
    fresh_keys = rotate(key_proj, positions).astype(jnp.bfloat16).reshape(NDOC, BLK, KVH * HD)
    fresh_values = value_proj.astype(jnp.bfloat16).reshape(NDOC, BLK, KVH * HD)
    return (fresh_keys, fresh_values)

def blend(stored, fresh, recompute_block):
    offsets = jnp.arange(DOCLEN, dtype=jnp.int32)[None, :] - recompute_block[:, None] * BLK
    inside = (offsets >= 0) & (offsets < BLK)
    picks = jnp.clip(offsets, 0, BLK - 1).astype(jnp.int32)
    chosen = jax.vmap(lambda rows_of, row_ids: rows_of[row_ids])(fresh, picks)
    return jnp.where(inside[:, :, None], chosen, stored)

def reference(hidden_rows, norm_gain, key_weight, value_weight, recompute_block, cache_keys, cache_values, slot_of_doc, session_docs, session_count, turn_queries, turn_keys, turn_values, turn_length):
    fresh_keys, fresh_values = recompute(hidden_rows, norm_gain, key_weight, value_weight, recompute_block)
    blended_keys = blend(cache_keys, fresh_keys, recompute_block)
    blended_values = blend(cache_values, fresh_values, recompute_block)

    def session(inputs):
        doc_ids, doc_count, queries, new_keys, new_values, length = inputs
        in_list = jnp.arange(DOCS_MAX, dtype=jnp.int32) < doc_count
        slots = slot_of_doc[jnp.where(in_list, doc_ids, 0)]
        doc_keys = blended_keys[slots].reshape(DOCS_MAX * DOCLEN, KVH, HD)
        doc_values = blended_values[slots].reshape(DOCS_MAX * DOCLEN, KVH, HD)
        key_rows = jnp.concatenate([doc_keys, new_keys.reshape(QLEN, KVH, HD)], axis=0)
        value_rows = jnp.concatenate([doc_values, new_values.reshape(QLEN, KVH, HD)], axis=0)
        query_ids = jnp.arange(QLEN, dtype=jnp.int32)
        doc_seen = jnp.broadcast_to(jnp.repeat(in_list, DOCLEN)[None, :], (QLEN, DOCS_MAX * DOCLEN))
        turn_seen = (query_ids[None, :] <= query_ids[:, None]) & (query_ids[None, :] < length)
        allowed = jnp.concatenate([doc_seen, turn_seen], axis=1)
        grouped = queries.reshape(QLEN, KVH, GQA, HD)

        def one_head(head_index):
            head_queries = lax.dynamic_index_in_dim(grouped, head_index, 1, keepdims=False).astype(jnp.float32)
            head_keys = lax.dynamic_index_in_dim(key_rows, head_index, 1, keepdims=False).astype(jnp.float32)
            head_values = lax.dynamic_index_in_dim(value_rows, head_index, 1, keepdims=False).astype(jnp.float32)
            scores = jnp.einsum('qgd,kd->gqk', head_queries, head_keys) * HD ** (-0.5)
            masked = jnp.where(allowed[None], scores, NEGATIVE)
            largest = lax.optimization_barrier(jnp.max(masked, axis=-1, keepdims=True))
            weights = jnp.where(allowed[None], jnp.exp(scores - largest), 0.0)
            row_total = lax.optimization_barrier(jnp.sum(weights, axis=-1))
            probs = weights.astype(jnp.bfloat16).astype(jnp.float32)
            summed = jnp.einsum('gqk,kd->gqd', probs, head_values)
            return summed / row_total[..., None]
        heads_out = lax.map(one_head, jnp.arange(KVH, dtype=jnp.int32))
        result = heads_out.transpose(2, 0, 1, 3).reshape(QLEN, QH * HD)
        result = jnp.where(query_ids[:, None] < length, result, 0.0)
        return result.astype(jnp.bfloat16)
    return lax.map(session, (session_docs, session_count, turn_queries, turn_keys, turn_values, turn_length))
```

```python
import jax
import jax.numpy as jnp
import numpy as np
from jax import lax
from jax.experimental import pallas as pl
from jax.experimental.pallas import tpu as pltpu
from jax.sharding import PartitionSpec as P

D = 8192
HD = 128
BLK = 128
QLEN = 128
GQA = 8


EPSILON = 1e-05
ROPE_BASE = 500000.0
NEGATIVE = -1e30


def rotate(values, positions):
    half_dim = values.shape[-1] // 2
    exponent = jnp.arange(half_dim, dtype=jnp.float32) * (2.0 / values.shape[-1])
    frequency = ROPE_BASE ** (-exponent)
    angles = positions.astype(jnp.float32)[..., None, None] * frequency
    cos_part = jnp.cos(angles)
    sin_part = jnp.sin(angles)
    first_half = values[..., :half_dim]
    second_half = values[..., half_dim:]
    return jnp.concatenate(
        [
            first_half * cos_part - second_half * sin_part,
            second_half * cos_part + first_half * sin_part,
        ],
        axis=-1,
    )


def attend(running, queries, key_rows, value_rows, allowed):
    run_max, run_sum, run_acc = running
    scores = jnp.einsum(
        "qhgd,khd->hgqk", queries, key_rows, preferred_element_type=jnp.float32
    ) * HD ** (-0.5)
    masked = jnp.where(allowed, scores, NEGATIVE)
    new_max = jnp.maximum(run_max, jnp.max(masked, axis=-1))
    weights = jnp.where(allowed, jnp.exp(scores - new_max[..., None]), 0.0)
    factor = jnp.exp(run_max - new_max)
    run_sum = run_sum * factor + jnp.sum(weights, axis=-1)
    update = jnp.einsum(
        "hgqk,khd->hgqd",
        weights.astype(jnp.bfloat16),
        value_rows,
        preferred_element_type=jnp.float32,
    )
    run_acc = run_acc * factor[..., None] + update
    return (new_max, run_sum, run_acc)


def split_page(one_page, kv_local):
    row_count = one_page.shape[0]
    key_rows = one_page[:, : kv_local * HD].reshape(row_count, kv_local, HD)
    value_rows = one_page[:, kv_local * HD :].reshape(row_count, kv_local, HD)
    return (key_rows, value_rows)


def local(
    hidden_rows,
    norm_gain,
    key_weight,
    value_weight,
    recompute_block,
    cache_keys,
    cache_values,
    slot_of_doc,
    session_docs,
    session_count,
    turn_queries,
    turn_keys,
    turn_values,
    turn_length,
):
    heads_here = lax.axis_size("heads")
    parts_sub = lax.axis_size("sub")
    half_index = lax.axis_index("sub")
    session = lax.axis_index("docs")
    docs_here, block_rows, local_width = hidden_rows.shape
    kv_local = cache_keys.shape[-1] // HD
    rows_half = block_rows // parts_sub
    half_rows = cache_keys.shape[1]
    docs_max = session_docs.shape[1]
    squares = jnp.sum(jnp.square(hidden_rows.astype(jnp.float32)), axis=-1)
    squares = lax.psum(squares, ("heads", "sub"))
    row_scale = lax.rsqrt(squares / D + EPSILON)
    scaled = (hidden_rows.astype(jnp.float32) * norm_gain.astype(jnp.float32)).astype(jnp.bfloat16)
    row_pieces = scaled.reshape(docs_here, parts_sub, rows_half, local_width)
    stacked_weights = jnp.stack(
        [
            key_weight.reshape(local_width, heads_here, kv_local * HD),
            value_weight.reshape(local_width, heads_here, kv_local * HD),
        ],
        axis=1,
    )
    partial_terms = jnp.einsum(
        "jsrd,dthc->hsjrtc", row_pieces, stacked_weights, preferred_element_type=jnp.float32
    )
    partial_terms = partial_terms.reshape(
        heads_here * parts_sub * docs_here * rows_half, 2 * kv_local * HD
    )
    own_rows = lax.psum_scatter(
        partial_terms.astype(jnp.bfloat16), ("heads", "sub"), scatter_dimension=0, tiled=True
    ).astype(jnp.float32)
    own_rows = own_rows.reshape(docs_here, rows_half, 2, kv_local, HD)
    own_scale = lax.dynamic_slice_in_dim(row_scale, half_index * rows_half, rows_half, 1)
    own_rows = own_rows * own_scale[:, :, None, None, None]
    row_ids = half_index * rows_half + jnp.arange(rows_half, dtype=jnp.int32)
    positions = recompute_block[:, None] * BLK + row_ids[None, :]
    new_keys = (
        rotate(own_rows[:, :, 0], positions)
        .astype(jnp.bfloat16)
        .reshape(docs_here, rows_half, kv_local * HD)
    )
    new_values = own_rows[:, :, 1].astype(jnp.bfloat16).reshape(docs_here, rows_half, kv_local * HD)
    fresh = jnp.concatenate([new_keys, new_values], axis=-1)
    fresh = lax.all_gather(fresh, "sub", axis=1, tiled=True)
    stored = jnp.concatenate([cache_keys, cache_values], axis=-1)
    global_rows = half_index * half_rows + jnp.arange(half_rows, dtype=jnp.int32)
    offsets = global_rows[None, :] - recompute_block[:, None] * BLK
    inside = (offsets >= 0) & (offsets < BLK)
    picks = jnp.clip(offsets, 0, BLK - 1)
    replaced = jax.vmap(lambda rows_of, row_picks: rows_of[row_picks])(fresh, picks)
    pages = jnp.where(inside[:, :, None], replaced, stored)
    my_docs = lax.dynamic_index_in_dim(session_docs, session, 0, keepdims=False)
    my_count = lax.dynamic_index_in_dim(session_count, session, 0, keepdims=False)
    in_list = jnp.arange(docs_max, dtype=jnp.int32) < my_count
    my_slots = jnp.where(in_list, slot_of_doc[jnp.where(in_list, my_docs, 0)], -1)
    length = turn_length[0]
    queries = turn_queries[0].reshape(QLEN, kv_local, GQA, HD)
    running = (
        jnp.full((kv_local, GQA, QLEN), NEGATIVE, jnp.float32),
        jnp.zeros((kv_local, GQA, QLEN), jnp.float32),
        jnp.zeros((kv_local, GQA, QLEN, HD), jnp.float32),
    )
    turn_rows = turn_keys.shape[1]
    key_ids = half_index * turn_rows + jnp.arange(turn_rows, dtype=jnp.int32)
    query_ids = jnp.arange(QLEN, dtype=jnp.int32)
    turn_seen = (key_ids[None, :] <= query_ids[:, None]) & (key_ids[None, :] < length)
    running = attend(
        running,
        queries,
        turn_keys[0].reshape(turn_rows, kv_local, HD),
        turn_values[0].reshape(turn_rows, kv_local, HD),
        turn_seen[None, None],
    )
    every_row = jnp.ones((1, 1, 1, half_rows), jnp.bool_)
    portion = lax.all_gather(pages, "docs", axis=0, tiled=True)

    def one_slot(position, inner_state):
        one_page = lax.dynamic_index_in_dim(portion, position, 0, keepdims=False)
        key_rows, value_rows = split_page(one_page, kv_local)
        wanted = jnp.any(my_slots == position)
        return lax.cond(
            wanted,
            lambda given: attend(given, queries, key_rows, value_rows, every_row),
            lambda given: given,
            inner_state,
        )

    running = lax.fori_loop(0, portion.shape[0], one_slot, running)
    run_max, run_sum, run_acc = running
    got_max, got_sum, got_acc = (
        lax.all_to_all(
            run_max.astype(jnp.bfloat16), "sub", split_axis=2, concat_axis=2, tiled=True
        ).astype(run_max.dtype),
        lax.all_to_all(
            run_sum.astype(jnp.bfloat16), "sub", split_axis=2, concat_axis=2, tiled=True
        ).astype(run_sum.dtype),
        lax.all_to_all(
            run_acc.astype(jnp.bfloat16), "sub", split_axis=2, concat_axis=2, tiled=True
        ).astype(run_acc.dtype),
    )
    query_half = QLEN // parts_sub
    got_max = got_max.reshape(kv_local, GQA, parts_sub, query_half)
    got_sum = got_sum.reshape(kv_local, GQA, parts_sub, query_half)
    got_acc = got_acc.reshape(kv_local, GQA, parts_sub, query_half, HD)
    joint_max = jnp.max(got_max, axis=2)
    source_weights = jnp.exp(got_max - joint_max[:, :, None, :])
    joint_sum = jnp.sum(got_sum * source_weights, axis=2)
    joint_acc = jnp.sum(got_acc * source_weights[..., None], axis=2)
    result = joint_acc / joint_sum[..., None]
    result = result.transpose(2, 0, 1, 3).reshape(query_half, kv_local * GQA * HD)
    own_queries = half_index * query_half + jnp.arange(query_half, dtype=jnp.int32)
    result = jnp.where(own_queries[:, None] < length, result, 0.0)
    return result.astype(jnp.bfloat16)[None]


def fused_kernel(
    docs_sm, count_sm, slot_sm, block_sm, length_sm,
    hidden_hbm, gain_ref, kw_hbm, vw_hbm, ck_hbm, cv_hbm, cos_hbm, sin_hbm, tq_hbm, tk_hbm, tv_hbm,
    out_ref,
    hid, scaled, wbuf, own, oth, turn, stage, kv, stage_fresh, kv_fresh, fresh, cos_t, sin_t,
    part_out, part_in, part_own, sq_out, sq_in, q_raw, q_all, run_max, run_sum, run_acc, o_send,
    load_sem, w_sem, chip_send, chip_recv, a_send, a_recv, b_send, b_recv, f_send, f_recv,
    p_send, p_recv, s_send, s_recv, o_sems,
):
    z = lax.axis_index("docs")
    h = lax.axis_index("heads")
    s = lax.axis_index("sub")
    n_docs = 4
    other = 1 - s
    mesh_id = pl.DeviceIdType.MESH
    pairs = [(1, 0), (1, 1), (0, 1), (0, 0)]

    def lanes(start, size):
        return pl.ds(pl.multiple_of(start, HD), size)

    my_cols = lanes(s * HD, HD)
    other_cols = lanes(other * HD, HD)

    loads = [
        (ck_hbm.at[:, :, my_cols], own.at[:, :, 0:HD]),
        (cv_hbm.at[:, :, my_cols], own.at[:, :, HD : 2 * HD]),
        (hidden_hbm, hid),
        (tq_hbm.at[0, :, lanes(s * GQA * HD, GQA * HD)], q_raw),
        (cos_hbm, cos_t),
        (sin_hbm, sin_t),
        (tk_hbm.at[0, :, my_cols], turn.at[s, :, 0:HD]),
        (tv_hbm.at[0, :, my_cols], turn.at[s, :, HD : 2 * HD]),
    ]
    loads = [
        pltpu.make_async_copy(src, dst, load_sem.at[i]) for i, (src, dst) in enumerate(loads)
    ]
    for i in (0, 1, 2):
        loads[i].start()
    w_loads = []
    for i, (dh, ds) in enumerate(pairs):
        head = 2 * lax.rem(h + dh, 2) + lax.rem(s + ds, 2)
        cols = lanes(head * HD, HD)
        w_loads.append(
            [
                pltpu.make_async_copy(kw_hbm.at[:, cols], wbuf.at[i, :, 0:HD], w_sem.at[2 * i]),
                pltpu.make_async_copy(
                    vw_hbm.at[:, cols], wbuf.at[i, :, HD : 2 * HD], w_sem.at[2 * i + 1]
                ),
            ]
        )
        for copy in w_loads[-1]:
            copy.start()
    for i in range(3, len(loads)):
        loads[i].start()

    barrier = pltpu.get_barrier_semaphore()
    for dh, ds in pairs[:3]:
        pl.semaphore_signal(
            barrier, inc=1,
            device_id={"heads": lax.rem(h + dh, 2), "sub": lax.rem(s + ds, 2)},
            device_id_type=mesh_id,
        )
    for d in range(1, n_docs):
        pl.semaphore_signal(
            barrier, inc=1, device_id={"docs": lax.rem(z + d, n_docs)}, device_id_type=mesh_id
        )
    pl.semaphore_wait(barrier, 6)

    def remote(src, dst, send, recv, device):
        copy = pltpu.make_async_remote_copy(
            src_ref=src, dst_ref=dst, send_sem=send, recv_sem=recv,
            device_id=device, device_id_type=mesh_id,
        )
        copy.start()
        return copy

    partner = {"sub": other}
    chip = [
        remote(ck_hbm.at[:, :, other_cols], oth.at[:, :, 0:HD], chip_send.at[0], chip_recv.at[0], partner),
        remote(cv_hbm.at[:, :, other_cols], oth.at[:, :, HD : 2 * HD], chip_send.at[1], chip_recv.at[1], partner),
        remote(tk_hbm.at[0, :, other_cols], turn.at[s, :, 0:HD], chip_send.at[2], chip_recv.at[2], partner),
        remote(tv_hbm.at[0, :, other_cols], turn.at[s, :, HD : 2 * HD], chip_send.at[3], chip_recv.at[3], partner),
    ]

    def reads(session, place):
        flag = jnp.int32(0)
        pick = jnp.int32(0)
        for k in range(docs_sm.shape[1]):
            listed = k < count_sm[session]
            doc = docs_sm[session, k]
            slot = jnp.int32(0)
            for j in range(slot_sm.shape[0]):
                slot = jnp.where(doc == j, slot_sm[j], slot)
            local_slot = slot - 2 * place
            hit = listed & (local_slot >= 0) & (local_slot < 2)
            flag = jnp.where(hit, 1, flag)
            pick = jnp.where(hit, local_slot, pick)
        return flag, pick

    picks = [reads(lax.rem(z + d, n_docs), z)[1] for d in range(n_docs)]
    bias = []
    for d in range(n_docs):
        flag, _ = reads(z, lax.rem(z + n_docs - d, n_docs))
        bias.append(jnp.where(flag == 1, jnp.float32(0.0), jnp.float32(NEGATIVE)))

    def choose(index, blocks):
        shape = blocks[0].shape
        wide = [block.astype(jnp.float32) for block in blocks]
        chosen = jnp.full(shape, index, jnp.int32)
        result = wide[0]
        for k in range(1, len(wide)):
            result = jnp.where(chosen == k, wide[k], result)
        return result.astype(blocks[0].dtype)

    loads[0].wait()
    loads[1].wait()
    order = (2, 1, 3, 0)
    holds, inner = [], []
    for d in range(n_docs):
        block = jnp.where(picks[d] == 1, block_sm[1], block_sm[0])
        upper = jnp.where(block >= 2, 1, 0)
        holds.append(upper == s)
        inner.append(block - 2 * upper)
    a_copies, b_copies, f_copies = {}, {}, {}
    for d in order:
        at = jnp.where(holds[d], 1 - inner[d], 0)
        rows = choose(picks[d] * 2 + at, [own[j, c * BLK : (c + 1) * BLK, :] for j in range(2) for c in range(2)])
        if d == 0:
            kv[0, 0:BLK, :] = rows
        else:
            stage[d - 1, 0:BLK, :] = rows
            a_copies[d] = remote(
                stage.at[d - 1, 0:BLK], kv.at[d, 0:BLK], a_send.at[d - 1], a_recv.at[d - 1],
                {"docs": lax.rem(z + d, n_docs)},
            )
    chip[0].wait_recv()
    chip[1].wait_recv()
    for d in order:
        at = jnp.where(holds[d], 0, 1 - inner[d])
        second = choose(picks[d] * 2 + at, [oth[j, c * BLK : (c + 1) * BLK, :] for j in range(2) for c in range(2)])
        third = choose(
            picks[d] * 2 + jnp.where(holds[d], 1, 0),
            [half_rows[j, BLK : 2 * BLK, :] for j in range(2) for half_rows in (own, oth)],
        )
        if d == 0:
            kv[0, BLK : 2 * BLK, :] = second
            kv[0, 2 * BLK : 3 * BLK, :] = third
        else:
            stage[d - 1, BLK : 2 * BLK, :] = second
            stage[d - 1, 2 * BLK : 3 * BLK, :] = third
            b_copies[d] = remote(
                stage.at[d - 1, BLK : 3 * BLK], kv.at[d, BLK : 3 * BLK],
                b_send.at[d - 1], b_recv.at[d - 1], {"docs": lax.rem(z + d, n_docs)},
            )

    loads[2].wait()
    width = hid.shape[-1]
    gain = gain_ref[...].astype(jnp.float32)
    sq_out[...] = jnp.zeros_like(sq_out)
    for j in range(2):
        total = jnp.zeros((BLK, HD), jnp.float32)
        for c in range(width // HD):
            cols = slice(c * HD, (c + 1) * HD)
            x = hid[j, :, cols].astype(jnp.float32)
            total = total + x * x
            scaled[j * BLK : (j + 1) * BLK, cols] = (x * gain[:, cols]).astype(jnp.bfloat16)
        sq_out[j : j + 1, :] = jnp.sum(total.T, axis=0, keepdims=True)
    p_copies, s_copies = [], []
    for i, (dh, ds) in enumerate(pairs):
        for copy in w_loads[i]:
            copy.wait()
        device = {"heads": lax.rem(h + dh, 2), "sub": lax.rem(s + ds, 2)}
        if i < 3:
            s_copies.append(remote(sq_out, sq_in.at[i], s_send.at[i], s_recv.at[i], device))
        term = jnp.dot(scaled[...], wbuf[i], preferred_element_type=jnp.float32)
        if i < 3:
            part_out[i] = term.astype(jnp.bfloat16)
            p_copies.append(
                remote(part_out.at[i], part_in.at[i], p_send.at[i], p_recv.at[i], device)
            )
        else:
            part_own[...] = term

    half = QLEN // 2
    loads[3].wait()
    for p in range(2):
        for head in range(GQA):
            at = (p * GQA + head) * half
            q_all[at : at + half, :] = q_raw[p * half : (p + 1) * half, head * HD : (head + 1) * HD]
    loads[6].wait()
    loads[7].wait()
    chip[2].wait_recv()
    chip[3].wait_recv()
    length = length_sm[0]
    scale = HD ** (-0.5)
    tile = 256

    def scores_of(at, key_rows):
        return lax.dot_general(
            q_all[pl.ds(at, tile), :], key_rows, (((1,), (1,)), ((), ())),
            preferred_element_type=jnp.float32,
        ) * scale

    def first(b, carry):
        at = pl.multiple_of(b * tile, tile)
        rows = turn[...].reshape(QLEN, 2 * HD)
        scores = scores_of(at, rows[:, 0:HD])
        row = lax.broadcasted_iota(jnp.int32, (tile, QLEN), 0)
        query = (row & (half - 1)) + (b // 2) * half
        key = lax.broadcasted_iota(jnp.int32, (tile, QLEN), 1)
        seen = (key <= query) & (key < length)
        scores = jnp.where(seen, scores, NEGATIVE)
        top = jnp.max(scores, axis=-1, keepdims=True)
        weights = jnp.exp(scores - top)
        run_max[pl.ds(at, tile), :] = top
        run_sum[pl.ds(at, tile), :] = jnp.sum(weights, axis=-1, keepdims=True)
        run_acc[pl.ds(at, tile), :] = jnp.dot(
            weights.astype(jnp.bfloat16), rows[:, HD : 2 * HD], preferred_element_type=jnp.float32
        )
        return carry

    def step(at, key_rows, value_rows, added):
        scores = scores_of(at, key_rows) + added
        before = run_max[pl.ds(at, tile), :]
        top = jnp.maximum(before, jnp.max(scores, axis=-1, keepdims=True))
        weights = jnp.exp(scores - top)
        factor = jnp.exp(before - top)
        row_sum = run_sum[pl.ds(at, tile), :] * factor + jnp.sum(weights, axis=-1, keepdims=True)
        acc = run_acc[pl.ds(at, tile), :] * factor + jnp.dot(
            weights.astype(jnp.bfloat16), value_rows, preferred_element_type=jnp.float32
        )
        return top, row_sum, acc

    def stored_step(d):
        def body(b, carry):
            at = pl.multiple_of(b * tile, tile)
            top, row_sum, acc = step(at, kv[d, :, 0:HD], kv[d, :, HD : 2 * HD], bias[d])
            run_max[pl.ds(at, tile), :] = top
            run_sum[pl.ds(at, tile), :] = row_sum
            run_acc[pl.ds(at, tile), :] = acc
            return carry

        lax.fori_loop(0, q_all.shape[0] // tile, body, 0)

    lax.fori_loop(0, q_all.shape[0] // tile, first, 0)
    stored_step(0)

    loads[4].wait()
    loads[5].wait()
    for copy in s_copies:
        copy.wait_recv()
    for copy in p_copies:
        copy.wait_recv()
    squares = sq_out[...]
    for i in range(3):
        squares = squares + sq_in[i]
    row_scale = lax.rsqrt(squares / D + EPSILON)
    for j in range(2):
        rows = slice(j * BLK, (j + 1) * BLK)
        term = part_own[rows, :]
        for i in range(3):
            term = term + part_in[i, rows, :].astype(jnp.float32)
        factor = jnp.broadcast_to(row_scale[j : j + 1, :], (BLK, HD)).T
        keys = term[:, 0:HD] * factor
        cos_rows = choose(block_sm[j], [cos_t[k * BLK : (k + 1) * BLK, :] for k in range(4)])
        sin_rows = choose(block_sm[j], [sin_t[k * BLK : (k + 1) * BLK, :] for k in range(4)])
        turned = keys * cos_rows + pltpu.roll(keys, HD // 2, 1) * sin_rows
        fresh[j, :, 0:HD] = turned.astype(jnp.bfloat16)
        fresh[j, :, HD : 2 * HD] = (term[:, HD : 2 * HD] * factor).astype(jnp.bfloat16)
    for d in order:
        rows = choose(picks[d], [fresh[0], fresh[1]])
        if d == 0:
            kv_fresh[0] = rows
        else:
            stage_fresh[d - 1] = rows
            f_copies[d] = remote(
                stage_fresh.at[d - 1], kv_fresh.at[d], f_send.at[d - 1], f_recv.at[d - 1],
                {"docs": lax.rem(z + d, n_docs)},
            )

    for d in (1, 3, 2):
        a_copies[d].wait_recv()
        b_copies[d].wait_recv()
        stored_step(d)
    for d in (1, 3, 2):
        f_copies[d].wait_recv()

    source = lax.broadcasted_iota(jnp.int32, (1, n_docs * BLK), 1)
    added = jnp.full((1, n_docs * BLK), bias[0], jnp.float32)
    for d in range(1, n_docs):
        added = jnp.where(source >= d * BLK, bias[d], added)
    rows_all = n_docs * BLK
    half_rows = GQA * half
    heads_tile = tile // half
    o_copy = None
    for turn_of in range(2):
        p = other if turn_of == 0 else s
        for b in range(half_rows // tile):
            at = pl.multiple_of(p * half_rows + b * tile, tile)
            pages = kv_fresh[...].reshape(rows_all, 2 * HD)
            top, row_sum, acc = step(at, pages[:, 0:HD], pages[:, HD : 2 * HD], added)
            result = (acc / row_sum).astype(jnp.bfloat16)
            for k in range(heads_tile):
                piece = result[k * half : (k + 1) * half, :]
                head = b * heads_tile + k
                if turn_of == 0:
                    o_send[:, head * HD : (head + 1) * HD] = piece
                else:
                    out_ref[:, lanes(s * GQA * HD + head * HD, HD)] = piece
        if turn_of == 0:
            o_copy = remote(o_send, out_ref.at[:, lanes(s * GQA * HD, GQA * HD)], o_sems.at[0], o_sems.at[1], partner)

    for copy in chip + s_copies + p_copies:
        copy.wait_send()
    for d in range(1, n_docs):
        a_copies[d].wait_send()
        b_copies[d].wait_send()
        f_copies[d].wait_send()
    o_copy.wait()


def fused(
    hidden_rows, norm_gain, key_weight, value_weight, recompute_block, cache_keys, cache_values,
    slot_of_doc, session_docs, session_count, turn_queries, turn_keys, turn_values, turn_length,
):
    width = hidden_rows.shape[-1]
    half = QLEN // 2
    rows = np.arange(4 * BLK, dtype=np.float64)[:, None]
    angles = rows * ROPE_BASE ** (-np.arange(HD // 2, dtype=np.float64) * 2.0 / HD)[None, :]
    cos_table = np.concatenate([np.cos(angles)] * 2, axis=1).astype(np.float32)
    sin_table = np.concatenate([-np.sin(angles), np.sin(angles)], axis=1).astype(np.float32)
    smem = pl.BlockSpec(memory_space=pltpu.SMEM)
    vmem = pl.BlockSpec(memory_space=pltpu.VMEM)
    hbm = pl.BlockSpec(memory_space=pltpu.HBM)
    bf, f32 = jnp.bfloat16, jnp.float32
    dma = pltpu.SemaphoreType.DMA
    result = pl.pallas_call(
        fused_kernel,
        out_shape=jax.ShapeDtypeStruct((half, 2 * GQA * HD), bf),
        in_specs=[smem] * 5 + [hbm, vmem] + [hbm] * 9,
        out_specs=vmem,
        scratch_shapes=[
            pltpu.VMEM((2, BLK, width), bf),
            pltpu.VMEM((2 * BLK, width), bf),
            pltpu.VMEM((4, width, 2 * HD), bf),
            pltpu.VMEM((2, 2 * BLK, 2 * HD), bf),
            pltpu.VMEM((2, 2 * BLK, 2 * HD), bf),
            pltpu.VMEM((2, half, 2 * HD), bf),
            pltpu.VMEM((3, 3 * BLK, 2 * HD), bf),
            pltpu.VMEM((4, 3 * BLK, 2 * HD), bf),
            pltpu.VMEM((3, BLK, 2 * HD), bf),
            pltpu.VMEM((4, BLK, 2 * HD), bf),
            pltpu.VMEM((2, BLK, 2 * HD), bf),
            pltpu.VMEM((4 * BLK, HD), f32),
            pltpu.VMEM((4 * BLK, HD), f32),
            pltpu.VMEM((3, 2 * BLK, 2 * HD), bf),
            pltpu.VMEM((3, 2 * BLK, 2 * HD), bf),
            pltpu.VMEM((2 * BLK, 2 * HD), f32),
            pltpu.VMEM((8, BLK), f32),
            pltpu.VMEM((3, 8, BLK), f32),
            pltpu.VMEM((QLEN, GQA * HD), bf),
            pltpu.VMEM((QLEN * GQA, HD), bf),
            pltpu.VMEM((QLEN * GQA, 1), f32),
            pltpu.VMEM((QLEN * GQA, 1), f32),
            pltpu.VMEM((QLEN * GQA, HD), f32),
            pltpu.VMEM((half, GQA * HD), bf),
            dma((8,)), dma((8,)), dma((4,)), dma((4,)),
            dma((3,)), dma((3,)), dma((3,)), dma((3,)), dma((3,)), dma((3,)),
            dma((3,)), dma((3,)), dma((3,)), dma((3,)), dma((2,)),
        ],
        compiler_params=pltpu.CompilerParams(
            collective_id=0, has_side_effects=True, vmem_limit_bytes=48 * 1024 * 1024
        ),
        cost_estimate=pl.CostEstimate(
            flops=2_500_000_000, bytes_accessed=8_000_000, transcendentals=3_000_000
        ),
    )(
        session_docs, session_count, slot_of_doc, recompute_block, turn_length,
        hidden_rows, norm_gain.reshape(1, width), key_weight, value_weight, cache_keys, cache_values,
        jnp.asarray(cos_table), jnp.asarray(sin_table), turn_queries, turn_keys, turn_values,
    )
    own_queries = lax.axis_index("sub") * half + jnp.arange(half, dtype=jnp.int32)
    return jnp.where(own_queries[:, None] < turn_length[0], result, jnp.bfloat16(0.0))[None]


def solution(mesh):
    in_specs = (
        P(("parts", "docs"), None, ("heads", "sub")),
        P(("heads", "sub")),
        P(("heads", "sub"), None),
        P(("heads", "sub"), None),
        P(("parts", "docs")),
        P(("parts", "docs"), "sub", "heads"),
        P(("parts", "docs"), "sub", "heads"),
        P("parts"),
        P("parts", None),
        P("parts"),
        P(("parts", "docs"), None, "heads"),
        P(("parts", "docs"), "sub", "heads"),
        P(("parts", "docs"), "sub", "heads"),
        P(("parts", "docs")),
    )
    out_specs = P(("parts", "docs"), "sub", "heads")
    sizes = tuple(mesh.shape[name] for name in ("docs", "heads", "sub"))
    chosen = fused if sizes == (4, 2, 2) else local
    return jax.shard_map(chosen, mesh=mesh, in_specs=in_specs, out_specs=out_specs, check_vma=False)
```

```python
import jax
import jax.numpy as jnp
import numpy as np
from jax import lax
from jax.experimental import pallas as pl
from jax.experimental.pallas import tpu as pltpu
from jax.sharding import PartitionSpec as P

D = 8192
HD = 128
BLK = 128
QLEN = 128
GQA = 8


EPSILON = 1e-05
ROPE_BASE = 500000.0
NEGATIVE = -1e30


def rotate(values, positions):
    half_dim = values.shape[-1] // 2
    exponent = jnp.arange(half_dim, dtype=jnp.float32) * (2.0 / values.shape[-1])
    frequency = ROPE_BASE ** (-exponent)
    angles = positions.astype(jnp.float32)[..., None, None] * frequency
    cos_part = jnp.cos(angles)
    sin_part = jnp.sin(angles)
    first_half = values[..., :half_dim]
    second_half = values[..., half_dim:]
    return jnp.concatenate(
        [
            first_half * cos_part - second_half * sin_part,
            second_half * cos_part + first_half * sin_part,
        ],
        axis=-1,
    )


def attend(running, queries, key_rows, value_rows, allowed):
    run_max, run_sum, run_acc = running
    scores = jnp.einsum(
        "qhgd,khd->hgqk", queries, key_rows, preferred_element_type=jnp.float32
    ) * HD ** (-0.5)
    masked = jnp.where(allowed, scores, NEGATIVE)
    new_max = jnp.maximum(run_max, jnp.max(masked, axis=-1))
    weights = jnp.where(allowed, jnp.exp(scores - new_max[..., None]), 0.0)
    factor = jnp.exp(run_max - new_max)
    run_sum = run_sum * factor + jnp.sum(weights, axis=-1)
    update = jnp.einsum(
        "hgqk,khd->hgqd",
        weights.astype(jnp.bfloat16),
        value_rows,
        preferred_element_type=jnp.float32,
    )
    run_acc = run_acc * factor[..., None] + update
    return (new_max, run_sum, run_acc)


def split_page(one_page, kv_local):
    row_count = one_page.shape[0]
    key_rows = one_page[:, : kv_local * HD].reshape(row_count, kv_local, HD)
    value_rows = one_page[:, kv_local * HD :].reshape(row_count, kv_local, HD)
    return (key_rows, value_rows)


def local(
    hidden_rows,
    norm_gain,
    key_weight,
    value_weight,
    recompute_block,
    cache_keys,
    cache_values,
    slot_of_doc,
    session_docs,
    session_count,
    turn_queries,
    turn_keys,
    turn_values,
    turn_length,
):
    heads_here = lax.axis_size("heads")
    parts_sub = lax.axis_size("sub")
    half_index = lax.axis_index("sub")
    session = lax.axis_index("docs")
    docs_here, block_rows, local_width = hidden_rows.shape
    kv_local = cache_keys.shape[-1] // HD
    rows_half = block_rows // parts_sub
    half_rows = cache_keys.shape[1]
    docs_max = session_docs.shape[1]
    squares = jnp.sum(jnp.square(hidden_rows.astype(jnp.float32)), axis=-1)
    squares = lax.psum(squares, ("heads", "sub"))
    row_scale = lax.rsqrt(squares / D + EPSILON)
    scaled = (hidden_rows.astype(jnp.float32) * norm_gain.astype(jnp.float32)).astype(jnp.bfloat16)
    row_pieces = scaled.reshape(docs_here, parts_sub, rows_half, local_width)
    stacked_weights = jnp.stack(
        [
            key_weight.reshape(local_width, heads_here, kv_local * HD),
            value_weight.reshape(local_width, heads_here, kv_local * HD),
        ],
        axis=1,
    )
    partial_terms = jnp.einsum(
        "jsrd,dthc->hsjrtc", row_pieces, stacked_weights, preferred_element_type=jnp.float32
    )
    partial_terms = partial_terms.reshape(
        heads_here * parts_sub * docs_here * rows_half, 2 * kv_local * HD
    )
    own_rows = lax.psum_scatter(
        partial_terms.astype(jnp.bfloat16), ("heads", "sub"), scatter_dimension=0, tiled=True
    ).astype(jnp.float32)
    own_rows = own_rows.reshape(docs_here, rows_half, 2, kv_local, HD)
    own_scale = lax.dynamic_slice_in_dim(row_scale, half_index * rows_half, rows_half, 1)
    own_rows = own_rows * own_scale[:, :, None, None, None]
    row_ids = half_index * rows_half + jnp.arange(rows_half, dtype=jnp.int32)
    positions = recompute_block[:, None] * BLK + row_ids[None, :]
    new_keys = (
        rotate(own_rows[:, :, 0], positions)
        .astype(jnp.bfloat16)
        .reshape(docs_here, rows_half, kv_local * HD)
    )
    new_values = own_rows[:, :, 1].astype(jnp.bfloat16).reshape(docs_here, rows_half, kv_local * HD)
    fresh = jnp.concatenate([new_keys, new_values], axis=-1)
    fresh = lax.all_gather(fresh, "sub", axis=1, tiled=True)
    stored = jnp.concatenate([cache_keys, cache_values], axis=-1)
    global_rows = half_index * half_rows + jnp.arange(half_rows, dtype=jnp.int32)
    offsets = global_rows[None, :] - recompute_block[:, None] * BLK
    inside = (offsets >= 0) & (offsets < BLK)
    picks = jnp.clip(offsets, 0, BLK - 1)
    replaced = jax.vmap(lambda rows_of, row_picks: rows_of[row_picks])(fresh, picks)
    pages = jnp.where(inside[:, :, None], replaced, stored)
    my_docs = lax.dynamic_index_in_dim(session_docs, session, 0, keepdims=False)
    my_count = lax.dynamic_index_in_dim(session_count, session, 0, keepdims=False)
    in_list = jnp.arange(docs_max, dtype=jnp.int32) < my_count
    my_slots = jnp.where(in_list, slot_of_doc[jnp.where(in_list, my_docs, 0)], -1)
    length = turn_length[0]
    queries = turn_queries[0].reshape(QLEN, kv_local, GQA, HD)
    running = (
        jnp.full((kv_local, GQA, QLEN), NEGATIVE, jnp.float32),
        jnp.zeros((kv_local, GQA, QLEN), jnp.float32),
        jnp.zeros((kv_local, GQA, QLEN, HD), jnp.float32),
    )
    turn_rows = turn_keys.shape[1]
    key_ids = half_index * turn_rows + jnp.arange(turn_rows, dtype=jnp.int32)
    query_ids = jnp.arange(QLEN, dtype=jnp.int32)
    turn_seen = (key_ids[None, :] <= query_ids[:, None]) & (key_ids[None, :] < length)
    running = attend(
        running,
        queries,
        turn_keys[0].reshape(turn_rows, kv_local, HD),
        turn_values[0].reshape(turn_rows, kv_local, HD),
        turn_seen[None, None],
    )
    every_row = jnp.ones((1, 1, 1, half_rows), jnp.bool_)
    portion = lax.all_gather(pages, "docs", axis=0, tiled=True)

    def one_slot(position, inner_state):
        one_page = lax.dynamic_index_in_dim(portion, position, 0, keepdims=False)
        key_rows, value_rows = split_page(one_page, kv_local)
        wanted = jnp.any(my_slots == position)
        return lax.cond(
            wanted,
            lambda given: attend(given, queries, key_rows, value_rows, every_row),
            lambda given: given,
            inner_state,
        )

    running = lax.fori_loop(0, portion.shape[0], one_slot, running)
    run_max, run_sum, run_acc = running
    got_max, got_sum, got_acc = (
        lax.all_to_all(
            run_max.astype(jnp.bfloat16), "sub", split_axis=2, concat_axis=2, tiled=True
        ).astype(run_max.dtype),
        lax.all_to_all(
            run_sum.astype(jnp.bfloat16), "sub", split_axis=2, concat_axis=2, tiled=True
        ).astype(run_sum.dtype),
        lax.all_to_all(
            run_acc.astype(jnp.bfloat16), "sub", split_axis=2, concat_axis=2, tiled=True
        ).astype(run_acc.dtype),
    )
    query_half = QLEN // parts_sub
    got_max = got_max.reshape(kv_local, GQA, parts_sub, query_half)
    got_sum = got_sum.reshape(kv_local, GQA, parts_sub, query_half)
    got_acc = got_acc.reshape(kv_local, GQA, parts_sub, query_half, HD)
    joint_max = jnp.max(got_max, axis=2)
    source_weights = jnp.exp(got_max - joint_max[:, :, None, :])
    joint_sum = jnp.sum(got_sum * source_weights, axis=2)
    joint_acc = jnp.sum(got_acc * source_weights[..., None], axis=2)
    result = joint_acc / joint_sum[..., None]
    result = result.transpose(2, 0, 1, 3).reshape(query_half, kv_local * GQA * HD)
    own_queries = half_index * query_half + jnp.arange(query_half, dtype=jnp.int32)
    result = jnp.where(own_queries[:, None] < length, result, 0.0)
    return result.astype(jnp.bfloat16)[None]


def fused_kernel(
    docs_sm, count_sm, slot_sm, block_sm, length_sm,
    hidden_hbm, gain_ref, kw_hbm, vw_hbm, ck_hbm, cv_hbm, cos_hbm, sin_hbm, tq_hbm, tk_hbm, tv_hbm,
    out_ref,
    hid, scaled, wbuf, own, oth, turn, stage, kv, stage_fresh, kv_fresh, fresh, cos_t, sin_t,
    part_out, part_in, part_own, sq_out, sq_in, q_raw, q_all, run_max, run_sum, run_acc, o_send,
    load_sem, w_sem, chip_send, chip_recv, a_send, a_recv, b_send, b_recv, f_send, f_recv,
    p_send, p_recv, s_send, s_recv, o_sems,
):
    z = lax.axis_index("docs")
    h = lax.axis_index("heads")
    s = lax.axis_index("sub")
    n_docs = 4
    other = 1 - s
    mesh_id = pl.DeviceIdType.MESH
    pairs = [(1, 0), (1, 1), (0, 1), (0, 0)]

    def lanes(start, size):
        return pl.ds(pl.multiple_of(start, HD), size)

    my_cols = lanes(s * HD, HD)
    other_cols = lanes(other * HD, HD)

    loads = [
        (ck_hbm.at[:, :, my_cols], own.at[:, :, 0:HD]),
        (cv_hbm.at[:, :, my_cols], own.at[:, :, HD : 2 * HD]),
        (hidden_hbm, hid),
        (tq_hbm.at[0, :, lanes(s * GQA * HD, GQA * HD)], q_raw),
        (cos_hbm, cos_t),
        (sin_hbm, sin_t),
        (tk_hbm.at[0, :, my_cols], turn.at[s, :, 0:HD]),
        (tv_hbm.at[0, :, my_cols], turn.at[s, :, HD : 2 * HD]),
    ]
    loads = [
        pltpu.make_async_copy(src, dst, load_sem.at[i]) for i, (src, dst) in enumerate(loads)
    ]
    for i in (0, 1, 2):
        loads[i].start()
    w_loads = []
    for i, (dh, ds) in enumerate(pairs):
        head = 2 * lax.rem(h + dh, 2) + lax.rem(s + ds, 2)
        cols = lanes(head * HD, HD)
        w_loads.append(
            [
                pltpu.make_async_copy(kw_hbm.at[:, cols], wbuf.at[i, :, 0:HD], w_sem.at[2 * i]),
                pltpu.make_async_copy(
                    vw_hbm.at[:, cols], wbuf.at[i, :, HD : 2 * HD], w_sem.at[2 * i + 1]
                ),
            ]
        )
        for copy in w_loads[-1]:
            copy.start()
    for i in range(3, len(loads)):
        loads[i].start()

    barrier = pltpu.get_barrier_semaphore()
    for dh, ds in pairs[:3]:
        pl.semaphore_signal(
            barrier, inc=1,
            device_id={"heads": lax.rem(h + dh, 2), "sub": lax.rem(s + ds, 2)},
            device_id_type=mesh_id,
        )
    for d in range(1, n_docs):
        pl.semaphore_signal(
            barrier, inc=1, device_id={"docs": lax.rem(z + d, n_docs)}, device_id_type=mesh_id
        )
    pl.semaphore_wait(barrier, 6)

    def remote(src, dst, send, recv, device):
        copy = pltpu.make_async_remote_copy(
            src_ref=src, dst_ref=dst, send_sem=send, recv_sem=recv,
            device_id=device, device_id_type=mesh_id,
        )
        copy.start()
        return copy

    partner = {"sub": other}
    chip = [
        remote(ck_hbm.at[:, :, other_cols], oth.at[:, :, 0:HD], chip_send.at[0], chip_recv.at[0], partner),
        remote(cv_hbm.at[:, :, other_cols], oth.at[:, :, HD : 2 * HD], chip_send.at[1], chip_recv.at[1], partner),
        remote(tk_hbm.at[0, :, other_cols], turn.at[s, :, 0:HD], chip_send.at[2], chip_recv.at[2], partner),
        remote(tv_hbm.at[0, :, other_cols], turn.at[s, :, HD : 2 * HD], chip_send.at[3], chip_recv.at[3], partner),
    ]

    def reads(session, place):
        flag = jnp.int32(0)
        pick = jnp.int32(0)
        for k in range(docs_sm.shape[1]):
            listed = k < count_sm[session]
            doc = docs_sm[session, k]
            slot = jnp.int32(0)
            for j in range(slot_sm.shape[0]):
                slot = jnp.where(doc == j, slot_sm[j], slot)
            local_slot = slot - 2 * place
            hit = listed & (local_slot >= 0) & (local_slot < 2)
            flag = jnp.where(hit, 1, flag)
            pick = jnp.where(hit, local_slot, pick)
        return flag, pick

    picks = [reads(lax.rem(z + d, n_docs), z)[1] for d in range(n_docs)]
    bias = []
    for d in range(n_docs):
        flag, _ = reads(z, lax.rem(z + n_docs - d, n_docs))
        bias.append(jnp.where(flag == 1, jnp.float32(0.0), jnp.float32(NEGATIVE)))

    def choose(index, blocks):
        shape = blocks[0].shape
        wide = [block.astype(jnp.float32) for block in blocks]
        chosen = jnp.full(shape, index, jnp.int32)
        result = wide[0]
        for k in range(1, len(wide)):
            result = jnp.where(chosen == k, wide[k], result)
        return result.astype(blocks[0].dtype)

    loads[0].wait()
    loads[1].wait()
    order = (2, 1, 3, 0)
    holds, inner = [], []
    for d in range(n_docs):
        block = jnp.where(picks[d] == 1, block_sm[1], block_sm[0])
        upper = jnp.where(block >= 2, 1, 0)
        holds.append(upper == s)
        inner.append(block - 2 * upper)
    a_copies, b_copies, f_copies = {}, {}, {}
    for d in order:
        at = jnp.where(holds[d], 1 - inner[d], 0)
        rows = choose(picks[d] * 2 + at, [own[j, c * BLK : (c + 1) * BLK, :] for j in range(2) for c in range(2)])
        if d == 0:
            kv[0, 0:BLK, :] = rows
        else:
            stage[d - 1, 0:BLK, :] = rows
            a_copies[d] = remote(
                stage.at[d - 1, 0:BLK], kv.at[d, 0:BLK], a_send.at[d - 1], a_recv.at[d - 1],
                {"docs": lax.rem(z + d, n_docs)},
            )
    chip[0].wait_recv()
    chip[1].wait_recv()
    for d in order:
        at = jnp.where(holds[d], 0, 1 - inner[d])
        second = choose(picks[d] * 2 + at, [oth[j, c * BLK : (c + 1) * BLK, :] for j in range(2) for c in range(2)])
        third = choose(
            picks[d] * 2 + jnp.where(holds[d], 1, 0),
            [half_rows[j, BLK : 2 * BLK, :] for j in range(2) for half_rows in (own, oth)],
        )
        if d == 0:
            kv[0, BLK : 2 * BLK, :] = second
            kv[0, 2 * BLK : 3 * BLK, :] = third
        else:
            stage[d - 1, BLK : 2 * BLK, :] = second
            stage[d - 1, 2 * BLK : 3 * BLK, :] = third
            b_copies[d] = remote(
                stage.at[d - 1, BLK : 3 * BLK], kv.at[d, BLK : 3 * BLK],
                b_send.at[d - 1], b_recv.at[d - 1], {"docs": lax.rem(z + d, n_docs)},
            )

    loads[2].wait()
    width = hid.shape[-1]
    gain = gain_ref[...].astype(jnp.float32)
    sq_out[...] = jnp.zeros_like(sq_out)
    for j in range(2):
        total = jnp.zeros((BLK, HD), jnp.float32)
        for c in range(width // HD):
            cols = slice(c * HD, (c + 1) * HD)
            x = hid[j, :, cols].astype(jnp.float32)
            total = total + x * x
            scaled[j * BLK : (j + 1) * BLK, cols] = (x * gain[:, cols]).astype(jnp.bfloat16)
        sq_out[j : j + 1, :] = jnp.sum(total.T, axis=0, keepdims=True)
    p_copies, s_copies = [], []
    for i, (dh, ds) in enumerate(pairs):
        for copy in w_loads[i]:
            copy.wait()
        device = {"heads": lax.rem(h + dh, 2), "sub": lax.rem(s + ds, 2)}
        if i < 3:
            s_copies.append(remote(sq_out, sq_in.at[i], s_send.at[i], s_recv.at[i], device))
        term = jnp.dot(scaled[...], wbuf[i], preferred_element_type=jnp.float32)
        if i < 3:
            part_out[i] = term.astype(jnp.bfloat16)
            p_copies.append(
                remote(part_out.at[i], part_in.at[i], p_send.at[i], p_recv.at[i], device)
            )
        else:
            part_own[...] = term

    half = QLEN // 2
    loads[3].wait()
    for p in range(2):
        for head in range(GQA):
            at = (p * GQA + head) * half
            q_all[at : at + half, :] = q_raw[p * half : (p + 1) * half, head * HD : (head + 1) * HD]
    loads[6].wait()
    loads[7].wait()
    chip[2].wait_recv()
    chip[3].wait_recv()
    length = length_sm[0]
    scale = HD ** (-0.5)
    tile = 256

    def scores_of(at, key_rows):
        return lax.dot_general(
            q_all[pl.ds(at, tile), :], key_rows, (((1,), (1,)), ((), ())),
            preferred_element_type=jnp.float32,
        ) * scale

    def first(b, carry):
        at = pl.multiple_of(b * tile, tile)
        rows = turn[...].reshape(QLEN, 2 * HD)
        scores = scores_of(at, rows[:, 0:HD])
        row = lax.broadcasted_iota(jnp.int32, (tile, QLEN), 0)
        query = (row & (half - 1)) + (b // 2) * half
        key = lax.broadcasted_iota(jnp.int32, (tile, QLEN), 1)
        seen = (key <= query) & (key < length)
        scores = jnp.where(seen, scores, NEGATIVE)
        top = jnp.max(scores, axis=-1, keepdims=True)
        weights = jnp.exp(scores - top)
        run_max[pl.ds(at, tile), :] = top
        run_sum[pl.ds(at, tile), :] = jnp.sum(weights, axis=-1, keepdims=True)
        run_acc[pl.ds(at, tile), :] = jnp.dot(
            weights.astype(jnp.bfloat16), rows[:, HD : 2 * HD], preferred_element_type=jnp.float32
        )
        return carry

    def step(at, key_rows, value_rows, added):
        scores = scores_of(at, key_rows) + added
        before = run_max[pl.ds(at, tile), :]
        top = jnp.maximum(before, jnp.max(scores, axis=-1, keepdims=True))
        weights = jnp.exp(scores - top)
        factor = jnp.exp(before - top)
        row_sum = run_sum[pl.ds(at, tile), :] * factor + jnp.sum(weights, axis=-1, keepdims=True)
        acc = run_acc[pl.ds(at, tile), :] * factor + jnp.dot(
            weights.astype(jnp.bfloat16), value_rows, preferred_element_type=jnp.float32
        )
        return top, row_sum, acc

    def stored_step(d):
        def body(b, carry):
            at = pl.multiple_of(b * tile, tile)
            top, row_sum, acc = step(at, kv[d, :, 0:HD], kv[d, :, HD : 2 * HD], bias[d])
            run_max[pl.ds(at, tile), :] = top
            run_sum[pl.ds(at, tile), :] = row_sum
            run_acc[pl.ds(at, tile), :] = acc
            return carry

        lax.fori_loop(0, q_all.shape[0] // tile, body, 0)

    lax.fori_loop(0, q_all.shape[0] // tile, first, 0)
    stored_step(0)

    loads[4].wait()
    loads[5].wait()
    for copy in s_copies:
        copy.wait_recv()
    for copy in p_copies:
        copy.wait_recv()
    squares = sq_out[...]
    for i in range(3):
        squares = squares + sq_in[i]
    row_scale = lax.rsqrt(squares / D + EPSILON)
    for j in range(2):
        rows = slice(j * BLK, (j + 1) * BLK)
        term = part_own[rows, :]
        for i in range(3):
            term = term + part_in[i, rows, :].astype(jnp.float32)
        factor = jnp.broadcast_to(row_scale[j : j + 1, :], (BLK, HD)).T
        keys = term[:, 0:HD] * factor
        cos_rows = choose(block_sm[j], [cos_t[k * BLK : (k + 1) * BLK, :] for k in range(4)])
        sin_rows = choose(block_sm[j], [sin_t[k * BLK : (k + 1) * BLK, :] for k in range(4)])
        turned = keys * cos_rows + pltpu.roll(keys, HD // 2, 1) * sin_rows
        fresh[j, :, 0:HD] = turned.astype(jnp.bfloat16)
        fresh[j, :, HD : 2 * HD] = (term[:, HD : 2 * HD] * factor).astype(jnp.bfloat16)
    for d in order:
        rows = choose(picks[d], [fresh[0], fresh[1]])
        if d == 0:
            kv_fresh[0] = rows
        else:
            stage_fresh[d - 1] = rows
            f_copies[d] = remote(
                stage_fresh.at[d - 1], kv_fresh.at[d], f_send.at[d - 1], f_recv.at[d - 1],
                {"docs": lax.rem(z + d, n_docs)},
            )

    for d in (1, 3, 2):
        a_copies[d].wait_recv()
        b_copies[d].wait_recv()
        stored_step(d)
    for d in (1, 3, 2):
        f_copies[d].wait_recv()

    source = lax.broadcasted_iota(jnp.int32, (1, n_docs * BLK), 1)
    added = jnp.full((1, n_docs * BLK), bias[0], jnp.float32)
    for d in range(1, n_docs):
        added = jnp.where(source >= d * BLK, bias[d], added)
    rows_all = n_docs * BLK
    half_rows = GQA * half
    heads_tile = tile // half
    o_copy = None
    for turn_of in range(2):
        p = other if turn_of == 0 else s
        for b in range(half_rows // tile):
            at = pl.multiple_of(p * half_rows + b * tile, tile)
            pages = kv_fresh[...].reshape(rows_all, 2 * HD)
            top, row_sum, acc = step(at, pages[:, 0:HD], pages[:, HD : 2 * HD], added)
            result = (acc / row_sum).astype(jnp.bfloat16)
            for k in range(heads_tile):
                piece = result[k * half : (k + 1) * half, :]
                head = b * heads_tile + k
                if turn_of == 0:
                    o_send[:, head * HD : (head + 1) * HD] = piece
                else:
                    out_ref[:, lanes(s * GQA * HD + head * HD, HD)] = piece
        if turn_of == 0:
            o_copy = remote(o_send, out_ref.at[:, lanes(s * GQA * HD, GQA * HD)], o_sems.at[0], o_sems.at[1], partner)

    for copy in chip + s_copies + p_copies:
        copy.wait_send()
    for d in range(1, n_docs):
        a_copies[d].wait_send()
        b_copies[d].wait_send()
        f_copies[d].wait_send()
    o_copy.wait()


def fused(
    hidden_rows, norm_gain, key_weight, value_weight, recompute_block, cache_keys, cache_values,
    slot_of_doc, session_docs, session_count, turn_queries, turn_keys, turn_values, turn_length,
):
    width = hidden_rows.shape[-1]
    half = QLEN // 2
    rows = np.arange(4 * BLK, dtype=np.float64)[:, None]
    angles = rows * ROPE_BASE ** (-np.arange(HD // 2, dtype=np.float64) * 2.0 / HD)[None, :]
    cos_table = np.concatenate([np.cos(angles)] * 2, axis=1).astype(np.float32)
    sin_table = np.concatenate([-np.sin(angles), np.sin(angles)], axis=1).astype(np.float32)
    smem = pl.BlockSpec(memory_space=pltpu.SMEM)
    vmem = pl.BlockSpec(memory_space=pltpu.VMEM)
    hbm = pl.BlockSpec(memory_space=pltpu.HBM)
    bf, f32 = jnp.bfloat16, jnp.float32
    dma = pltpu.SemaphoreType.DMA
    result = pl.pallas_call(
        fused_kernel,
        out_shape=jax.ShapeDtypeStruct((half, 2 * GQA * HD), bf),
        in_specs=[smem] * 5 + [hbm, vmem] + [hbm] * 9,
        out_specs=vmem,
        scratch_shapes=[
            pltpu.VMEM((2, BLK, width), bf),
            pltpu.VMEM((2 * BLK, width), bf),
            pltpu.VMEM((4, width, 2 * HD), bf),
            pltpu.VMEM((2, 2 * BLK, 2 * HD), bf),
            pltpu.VMEM((2, 2 * BLK, 2 * HD), bf),
            pltpu.VMEM((2, half, 2 * HD), bf),
            pltpu.VMEM((3, 3 * BLK, 2 * HD), bf),
            pltpu.VMEM((4, 3 * BLK, 2 * HD), bf),
            pltpu.VMEM((3, BLK, 2 * HD), bf),
            pltpu.VMEM((4, BLK, 2 * HD), bf),
            pltpu.VMEM((2, BLK, 2 * HD), bf),
            pltpu.VMEM((4 * BLK, HD), f32),
            pltpu.VMEM((4 * BLK, HD), f32),
            pltpu.VMEM((3, 2 * BLK, 2 * HD), bf),
            pltpu.VMEM((3, 2 * BLK, 2 * HD), bf),
            pltpu.VMEM((2 * BLK, 2 * HD), f32),
            pltpu.VMEM((8, BLK), f32),
            pltpu.VMEM((3, 8, BLK), f32),
            pltpu.VMEM((QLEN, GQA * HD), bf),
            pltpu.VMEM((QLEN * GQA, HD), bf),
            pltpu.VMEM((QLEN * GQA, 1), f32),
            pltpu.VMEM((QLEN * GQA, 1), f32),
            pltpu.VMEM((QLEN * GQA, HD), f32),
            pltpu.VMEM((half, GQA * HD), bf),
            dma((8,)), dma((8,)), dma((4,)), dma((4,)),
            dma((3,)), dma((3,)), dma((3,)), dma((3,)), dma((3,)), dma((3,)),
            dma((3,)), dma((3,)), dma((3,)), dma((3,)), dma((2,)),
        ],
        compiler_params=pltpu.CompilerParams(
            collective_id=0, has_side_effects=True, vmem_limit_bytes=63 * 1024 * 1024
        ),
        cost_estimate=pl.CostEstimate(
            flops=2_500_000_000, bytes_accessed=8_000_000, transcendentals=3_000_000
        ),
    )(
        session_docs, session_count, slot_of_doc, recompute_block, turn_length,
        hidden_rows, norm_gain.reshape(1, width), key_weight, value_weight, cache_keys, cache_values,
        jnp.asarray(cos_table), jnp.asarray(sin_table), turn_queries, turn_keys, turn_values,
    )
    own_queries = lax.axis_index("sub") * half + jnp.arange(half, dtype=jnp.int32)
    return jnp.where(own_queries[:, None] < turn_length[0], result, jnp.bfloat16(0.0))[None]


def solution(mesh):
    in_specs = (
        P(("parts", "docs"), None, ("heads", "sub")),
        P(("heads", "sub")),
        P(("heads", "sub"), None),
        P(("heads", "sub"), None),
        P(("parts", "docs")),
        P(("parts", "docs"), "sub", "heads"),
        P(("parts", "docs"), "sub", "heads"),
        P("parts"),
        P("parts", None),
        P("parts"),
        P(("parts", "docs"), None, "heads"),
        P(("parts", "docs"), "sub", "heads"),
        P(("parts", "docs"), "sub", "heads"),
        P(("parts", "docs")),
    )
    out_specs = P(("parts", "docs"), "sub", "heads")
    sizes = tuple(mesh.shape[name] for name in ("docs", "heads", "sub"))
    chosen = fused if sizes == (4, 2, 2) else local
    return jax.shard_map(chosen, mesh=mesh, in_specs=in_specs, out_specs=out_specs, check_vma=False)
```

```python
import jax
import jax.numpy as jnp
import numpy as np
from jax import lax
from jax.experimental import pallas as pl
from jax.experimental.pallas import tpu as pltpu
from jax.sharding import PartitionSpec as P

D = 8192
HD = 128
BLK = 128
QLEN = 128
GQA = 8


EPSILON = 1e-05
ROPE_BASE = 500000.0
NEGATIVE = -1e30


def rotate(values, positions):
    half_dim = values.shape[-1] // 2
    exponent = jnp.arange(half_dim, dtype=jnp.float32) * (2.0 / values.shape[-1])
    frequency = ROPE_BASE ** (-exponent)
    angles = positions.astype(jnp.float32)[..., None, None] * frequency
    cos_part = jnp.cos(angles)
    sin_part = jnp.sin(angles)
    first_half = values[..., :half_dim]
    second_half = values[..., half_dim:]
    return jnp.concatenate(
        [
            first_half * cos_part - second_half * sin_part,
            second_half * cos_part + first_half * sin_part,
        ],
        axis=-1,
    )


def attend(running, queries, key_rows, value_rows, allowed):
    run_max, run_sum, run_acc = running
    scores = jnp.einsum(
        "qhgd,khd->hgqk", queries, key_rows, preferred_element_type=jnp.float32
    ) * HD ** (-0.5)
    masked = jnp.where(allowed, scores, NEGATIVE)
    new_max = jnp.maximum(run_max, jnp.max(masked, axis=-1))
    weights = jnp.where(allowed, jnp.exp(scores - new_max[..., None]), 0.0)
    factor = jnp.exp(run_max - new_max)
    run_sum = run_sum * factor + jnp.sum(weights, axis=-1)
    update = jnp.einsum(
        "hgqk,khd->hgqd",
        weights.astype(jnp.bfloat16),
        value_rows,
        preferred_element_type=jnp.float32,
    )
    run_acc = run_acc * factor[..., None] + update
    return (new_max, run_sum, run_acc)


def split_page(one_page, kv_local):
    row_count = one_page.shape[0]
    key_rows = one_page[:, : kv_local * HD].reshape(row_count, kv_local, HD)
    value_rows = one_page[:, kv_local * HD :].reshape(row_count, kv_local, HD)
    return (key_rows, value_rows)


def local(
    hidden_rows,
    norm_gain,
    key_weight,
    value_weight,
    recompute_block,
    cache_keys,
    cache_values,
    slot_of_doc,
    session_docs,
    session_count,
    turn_queries,
    turn_keys,
    turn_values,
    turn_length,
):
    heads_here = lax.axis_size("heads")
    parts_sub = lax.axis_size("sub")
    half_index = lax.axis_index("sub")
    session = lax.axis_index("docs")
    docs_here, block_rows, local_width = hidden_rows.shape
    kv_local = cache_keys.shape[-1] // HD
    rows_half = block_rows // parts_sub
    half_rows = cache_keys.shape[1]
    docs_max = session_docs.shape[1]
    squares = jnp.sum(jnp.square(hidden_rows.astype(jnp.float32)), axis=-1)
    squares = lax.psum(squares, ("heads", "sub"))
    row_scale = lax.rsqrt(squares / D + EPSILON)
    scaled = (hidden_rows.astype(jnp.float32) * norm_gain.astype(jnp.float32)).astype(jnp.bfloat16)
    row_pieces = scaled.reshape(docs_here, parts_sub, rows_half, local_width)
    stacked_weights = jnp.stack(
        [
            key_weight.reshape(local_width, heads_here, kv_local * HD),
            value_weight.reshape(local_width, heads_here, kv_local * HD),
        ],
        axis=1,
    )
    partial_terms = jnp.einsum(
        "jsrd,dthc->hsjrtc", row_pieces, stacked_weights, preferred_element_type=jnp.float32
    )
    partial_terms = partial_terms.reshape(
        heads_here * parts_sub * docs_here * rows_half, 2 * kv_local * HD
    )
    own_rows = lax.psum_scatter(
        partial_terms.astype(jnp.bfloat16), ("heads", "sub"), scatter_dimension=0, tiled=True
    ).astype(jnp.float32)
    own_rows = own_rows.reshape(docs_here, rows_half, 2, kv_local, HD)
    own_scale = lax.dynamic_slice_in_dim(row_scale, half_index * rows_half, rows_half, 1)
    own_rows = own_rows * own_scale[:, :, None, None, None]
    row_ids = half_index * rows_half + jnp.arange(rows_half, dtype=jnp.int32)
    positions = recompute_block[:, None] * BLK + row_ids[None, :]
    new_keys = (
        rotate(own_rows[:, :, 0], positions)
        .astype(jnp.bfloat16)
        .reshape(docs_here, rows_half, kv_local * HD)
    )
    new_values = own_rows[:, :, 1].astype(jnp.bfloat16).reshape(docs_here, rows_half, kv_local * HD)
    fresh = jnp.concatenate([new_keys, new_values], axis=-1)
    fresh = lax.all_gather(fresh, "sub", axis=1, tiled=True)
    stored = jnp.concatenate([cache_keys, cache_values], axis=-1)
    global_rows = half_index * half_rows + jnp.arange(half_rows, dtype=jnp.int32)
    offsets = global_rows[None, :] - recompute_block[:, None] * BLK
    inside = (offsets >= 0) & (offsets < BLK)
    picks = jnp.clip(offsets, 0, BLK - 1)
    replaced = jax.vmap(lambda rows_of, row_picks: rows_of[row_picks])(fresh, picks)
    pages = jnp.where(inside[:, :, None], replaced, stored)
    my_docs = lax.dynamic_index_in_dim(session_docs, session, 0, keepdims=False)
    my_count = lax.dynamic_index_in_dim(session_count, session, 0, keepdims=False)
    in_list = jnp.arange(docs_max, dtype=jnp.int32) < my_count
    my_slots = jnp.where(in_list, slot_of_doc[jnp.where(in_list, my_docs, 0)], -1)
    length = turn_length[0]
    queries = turn_queries[0].reshape(QLEN, kv_local, GQA, HD)
    running = (
        jnp.full((kv_local, GQA, QLEN), NEGATIVE, jnp.float32),
        jnp.zeros((kv_local, GQA, QLEN), jnp.float32),
        jnp.zeros((kv_local, GQA, QLEN, HD), jnp.float32),
    )
    turn_rows = turn_keys.shape[1]
    key_ids = half_index * turn_rows + jnp.arange(turn_rows, dtype=jnp.int32)
    query_ids = jnp.arange(QLEN, dtype=jnp.int32)
    turn_seen = (key_ids[None, :] <= query_ids[:, None]) & (key_ids[None, :] < length)
    running = attend(
        running,
        queries,
        turn_keys[0].reshape(turn_rows, kv_local, HD),
        turn_values[0].reshape(turn_rows, kv_local, HD),
        turn_seen[None, None],
    )
    every_row = jnp.ones((1, 1, 1, half_rows), jnp.bool_)
    portion = lax.all_gather(pages, "docs", axis=0, tiled=True)

    def one_slot(position, inner_state):
        one_page = lax.dynamic_index_in_dim(portion, position, 0, keepdims=False)
        key_rows, value_rows = split_page(one_page, kv_local)
        wanted = jnp.any(my_slots == position)
        return lax.cond(
            wanted,
            lambda given: attend(given, queries, key_rows, value_rows, every_row),
            lambda given: given,
            inner_state,
        )

    running = lax.fori_loop(0, portion.shape[0], one_slot, running)
    run_max, run_sum, run_acc = running
    got_max, got_sum, got_acc = (
        lax.all_to_all(
            run_max.astype(jnp.bfloat16), "sub", split_axis=2, concat_axis=2, tiled=True
        ).astype(run_max.dtype),
        lax.all_to_all(
            run_sum.astype(jnp.bfloat16), "sub", split_axis=2, concat_axis=2, tiled=True
        ).astype(run_sum.dtype),
        lax.all_to_all(
            run_acc.astype(jnp.bfloat16), "sub", split_axis=2, concat_axis=2, tiled=True
        ).astype(run_acc.dtype),
    )
    query_half = QLEN // parts_sub
    got_max = got_max.reshape(kv_local, GQA, parts_sub, query_half)
    got_sum = got_sum.reshape(kv_local, GQA, parts_sub, query_half)
    got_acc = got_acc.reshape(kv_local, GQA, parts_sub, query_half, HD)
    joint_max = jnp.max(got_max, axis=2)
    source_weights = jnp.exp(got_max - joint_max[:, :, None, :])
    joint_sum = jnp.sum(got_sum * source_weights, axis=2)
    joint_acc = jnp.sum(got_acc * source_weights[..., None], axis=2)
    result = joint_acc / joint_sum[..., None]
    result = result.transpose(2, 0, 1, 3).reshape(query_half, kv_local * GQA * HD)
    own_queries = half_index * query_half + jnp.arange(query_half, dtype=jnp.int32)
    result = jnp.where(own_queries[:, None] < length, result, 0.0)
    return result.astype(jnp.bfloat16)[None]


def fused_kernel(
    docs_sm, count_sm, slot_sm, block_sm, length_sm,
    hidden_hbm, gain_ref, kw_hbm, vw_hbm, ck_hbm, cv_hbm, cos_hbm, sin_hbm, tq_hbm, tk_hbm, tv_hbm,
    out_ref,
    hid, scaled, wbuf, own, oth, turn, stage, kv, stage_fresh, kv_fresh, fresh, cos_t, sin_t,
    part_out, part_in, part_own, sq_out, sq_in, q_raw, q_all, run_max, run_sum, run_acc, o_send,
    load_sem, w_sem, chip_send, chip_recv, a_send, a_recv, b_send, b_recv, f_send, f_recv,
    p_send, p_recv, s_send, s_recv, o_sems,
):
    z = lax.axis_index("docs")
    h = lax.axis_index("heads")
    s = lax.axis_index("sub")
    n_docs = 4
    other = 1 - s
    mesh_id = pl.DeviceIdType.MESH
    pairs = [(1, 0), (1, 1), (0, 1), (0, 0)]
    peers = [z, z + 1 - 2 * lax.rem(z, 2), lax.rem(z + 2, n_docs), 3 - z]

    def lanes(start, size):
        return pl.ds(pl.multiple_of(start, HD), size)

    my_cols = lanes(s * HD, HD)
    other_cols = lanes(other * HD, HD)

    barrier = pltpu.get_barrier_semaphore()
    for dh, ds in pairs[:3]:
        pl.semaphore_signal(
            barrier, inc=1,
            device_id={"heads": lax.rem(h + dh, 2), "sub": lax.rem(s + ds, 2)},
            device_id_type=mesh_id,
        )
    for d in range(1, n_docs):
        pl.semaphore_signal(
            barrier, inc=1, device_id={"docs": peers[d]}, device_id_type=mesh_id
        )

    loads = [
        (ck_hbm.at[:, :, my_cols], own.at[:, :, 0:HD]),
        (cv_hbm.at[:, :, my_cols], own.at[:, :, HD : 2 * HD]),
        (hidden_hbm, hid),
        (tq_hbm.at[0, :, lanes(s * GQA * HD, GQA * HD)], q_raw),
        (cos_hbm, cos_t),
        (sin_hbm, sin_t),
        (tk_hbm.at[0, :, my_cols], turn.at[s, :, 0:HD]),
        (tv_hbm.at[0, :, my_cols], turn.at[s, :, HD : 2 * HD]),
    ]
    loads = [
        pltpu.make_async_copy(src, dst, load_sem.at[i]) for i, (src, dst) in enumerate(loads)
    ]
    for i in (0, 1, 2):
        loads[i].start()
    w_loads = []
    for i, (dh, ds) in enumerate(pairs):
        head = 2 * lax.rem(h + dh, 2) + lax.rem(s + ds, 2)
        cols = lanes(head * HD, HD)
        w_loads.append(
            [
                pltpu.make_async_copy(kw_hbm.at[:, cols], wbuf.at[i, :, 0:HD], w_sem.at[2 * i]),
                pltpu.make_async_copy(
                    vw_hbm.at[:, cols], wbuf.at[i, :, HD : 2 * HD], w_sem.at[2 * i + 1]
                ),
            ]
        )
        for copy in w_loads[-1]:
            copy.start()
    for i in range(3, len(loads)):
        loads[i].start()

    def remote(src, dst, send, recv, device):
        copy = pltpu.make_async_remote_copy(
            src_ref=src, dst_ref=dst, send_sem=send, recv_sem=recv,
            device_id=device, device_id_type=mesh_id,
        )
        copy.start()
        return copy

    def reads(session, place):
        flag = jnp.int32(0)
        pick = jnp.int32(0)
        for k in range(docs_sm.shape[1]):
            listed = k < count_sm[session]
            doc = docs_sm[session, k]
            slot = jnp.int32(0)
            for j in range(slot_sm.shape[0]):
                slot = jnp.where(doc == j, slot_sm[j], slot)
            local_slot = slot - 2 * place
            hit = listed & (local_slot >= 0) & (local_slot < 2)
            flag = jnp.where(hit, 1, flag)
            pick = jnp.where(hit, local_slot, pick)
        return flag, pick

    picks = [reads(peers[d], z)[1] for d in range(n_docs)]
    bias = []
    for d in range(n_docs):
        flag, _ = reads(z, peers[d])
        bias.append(jnp.where(flag == 1, jnp.float32(0.0), jnp.float32(NEGATIVE)))

    def choose(index, blocks):
        shape = blocks[0].shape
        wide = [block.astype(jnp.float32) for block in blocks]
        chosen = jnp.full(shape, index, jnp.int32)
        result = wide[0]
        for k in range(1, len(wide)):
            result = jnp.where(chosen == k, wide[k], result)
        return result.astype(blocks[0].dtype)

    loads[0].wait()
    loads[1].wait()
    order = (1, 2, 3, 0)
    holds, inner = [], []
    for d in range(n_docs):
        block = jnp.where(picks[d] == 1, block_sm[1], block_sm[0])
        upper = jnp.where(block >= 2, 1, 0)
        holds.append(upper == s)
        inner.append(block - 2 * upper)
    a_copies, b_copies, f_copies = {}, {}, {}
    for d in order:
        at = jnp.where(holds[d], 1 - inner[d], 0)
        rows = choose(picks[d] * 2 + at, [own[j, c * BLK : (c + 1) * BLK, :] for j in range(2) for c in range(2)])
        if d == 0:
            kv[0, 0:BLK, :] = rows
        else:
            stage[d - 1, 0:BLK, :] = rows
    pl.semaphore_wait(barrier, 6)

    partner = {"sub": other}
    chip = [
        remote(ck_hbm.at[:, :, other_cols], oth.at[:, :, 0:HD], chip_send.at[0], chip_recv.at[0], partner),
        remote(cv_hbm.at[:, :, other_cols], oth.at[:, :, HD : 2 * HD], chip_send.at[1], chip_recv.at[1], partner),
        remote(tk_hbm.at[0, :, other_cols], turn.at[s, :, 0:HD], chip_send.at[2], chip_recv.at[2], partner),
        remote(tv_hbm.at[0, :, other_cols], turn.at[s, :, HD : 2 * HD], chip_send.at[3], chip_recv.at[3], partner),
    ]

    for d in (1, 2, 3):
        a_copies[d] = remote(
            stage.at[d - 1, 0:BLK], kv.at[d, 0:BLK], a_send.at[d - 1], a_recv.at[d - 1],
            {"docs": peers[d]},
        )
    chip[0].wait_recv()
    chip[1].wait_recv()
    for d in order:
        at = jnp.where(holds[d], 0, 1 - inner[d])
        second = choose(picks[d] * 2 + at, [oth[j, c * BLK : (c + 1) * BLK, :] for j in range(2) for c in range(2)])
        third = choose(
            picks[d] * 2 + jnp.where(holds[d], 1, 0),
            [half_rows[j, BLK : 2 * BLK, :] for j in range(2) for half_rows in (own, oth)],
        )
        if d == 0:
            kv[0, BLK : 2 * BLK, :] = second
            kv[0, 2 * BLK : 3 * BLK, :] = third
        else:
            stage[d - 1, BLK : 2 * BLK, :] = second
            stage[d - 1, 2 * BLK : 3 * BLK, :] = third
            b_copies[d] = remote(
                stage.at[d - 1, BLK : 3 * BLK], kv.at[d, BLK : 3 * BLK],
                b_send.at[d - 1], b_recv.at[d - 1], {"docs": peers[d]},
            )

    loads[2].wait()
    width = hid.shape[-1]
    gain = gain_ref[...].astype(jnp.float32).reshape(1, width)
    sq_out[...] = jnp.zeros_like(sq_out)
    for j in range(2):
        total = jnp.zeros((BLK, HD), jnp.float32)
        for c in range(width // HD):
            cols = slice(c * HD, (c + 1) * HD)
            x = hid[j, :, cols].astype(jnp.float32)
            total = total + x * x
            scaled[j * BLK : (j + 1) * BLK, cols] = (x * gain[:, cols]).astype(jnp.bfloat16)
        sq_out[j : j + 1, :] = jnp.sum(total.T, axis=0, keepdims=True)
    p_copies, s_copies = [], []
    for i, (dh, ds) in enumerate(pairs):
        for copy in w_loads[i]:
            copy.wait()
        device = {"heads": lax.rem(h + dh, 2), "sub": lax.rem(s + ds, 2)}
        if i < 3:
            s_copies.append(remote(sq_out, sq_in.at[i], s_send.at[i], s_recv.at[i], device))
        term = jnp.dot(scaled[...], wbuf[i], preferred_element_type=jnp.float32)
        if i < 3:
            part_out[i] = term.astype(jnp.bfloat16)
            p_copies.append(
                remote(part_out.at[i], part_in.at[i], p_send.at[i], p_recv.at[i], device)
            )
        else:
            part_own[...] = term

    half = QLEN // 2
    loads[3].wait()
    for p in range(2):
        for head in range(GQA):
            at = (p * GQA + head) * half
            q_all[at : at + half, :] = q_raw[p * half : (p + 1) * half, head * HD : (head + 1) * HD]
    loads[6].wait()
    loads[7].wait()
    chip[2].wait_recv()
    chip[3].wait_recv()
    length = length_sm[0]
    scale = HD ** (-0.5)
    tile = 256

    def scores_of(at, key_rows):
        return lax.dot_general(
            q_all[pl.ds(at, tile), :], key_rows, (((1,), (1,)), ((), ())),
            preferred_element_type=jnp.float32,
        ) * scale

    def first(b, carry):
        at = pl.multiple_of(b * tile, tile)
        rows = turn[...].reshape(QLEN, 2 * HD)
        scores = scores_of(at, rows[:, 0:HD])
        row = lax.broadcasted_iota(jnp.int32, (tile, QLEN), 0)
        query = (row & (half - 1)) + (b // 2) * half
        key = lax.broadcasted_iota(jnp.int32, (tile, QLEN), 1)
        seen = (key <= query) & (key < length)
        scores = jnp.where(seen, scores, NEGATIVE)
        top = jnp.max(scores, axis=-1, keepdims=True)
        weights = jnp.exp(scores - top)
        run_max[pl.ds(at, tile), :] = top
        run_sum[pl.ds(at, tile), :] = jnp.sum(weights, axis=-1, keepdims=True)
        run_acc[pl.ds(at, tile), :] = jnp.dot(
            weights.astype(jnp.bfloat16), rows[:, HD : 2 * HD], preferred_element_type=jnp.float32
        )
        return carry

    def step(at, key_rows, value_rows, added):
        scores = scores_of(at, key_rows) + added
        before = run_max[pl.ds(at, tile), :]
        top = jnp.maximum(before, jnp.max(scores, axis=-1, keepdims=True))
        weights = jnp.exp(scores - top)
        factor = jnp.exp(before - top)
        row_sum = run_sum[pl.ds(at, tile), :] * factor + jnp.sum(weights, axis=-1, keepdims=True)
        acc = run_acc[pl.ds(at, tile), :] * factor + jnp.dot(
            weights.astype(jnp.bfloat16), value_rows, preferred_element_type=jnp.float32
        )
        return top, row_sum, acc

    def stored_step(d):
        def body(b, carry):
            at = pl.multiple_of(b * tile, tile)
            top, row_sum, acc = step(at, kv[d, :, 0:HD], kv[d, :, HD : 2 * HD], bias[d])
            run_max[pl.ds(at, tile), :] = top
            run_sum[pl.ds(at, tile), :] = row_sum
            run_acc[pl.ds(at, tile), :] = acc
            return carry

        lax.fori_loop(0, q_all.shape[0] // tile, body, 0)

    lax.fori_loop(0, q_all.shape[0] // tile, first, 0)
    stored_step(0)

    loads[4].wait()
    loads[5].wait()
    for copy in s_copies:
        copy.wait_recv()
    for copy in p_copies:
        copy.wait_recv()
    squares = sq_out[...]
    for i in range(3):
        squares = squares + sq_in[i]
    row_scale = lax.rsqrt(squares / D + EPSILON)
    for j in range(2):
        rows = slice(j * BLK, (j + 1) * BLK)
        term = part_own[rows, :]
        for i in range(3):
            term = term + part_in[i, rows, :].astype(jnp.float32)
        factor = jnp.broadcast_to(row_scale[j : j + 1, :], (BLK, HD)).T
        keys = term[:, 0:HD] * factor
        cos_rows = choose(block_sm[j], [cos_t[k * BLK : (k + 1) * BLK, :] for k in range(4)])
        sin_rows = choose(block_sm[j], [sin_t[k * BLK : (k + 1) * BLK, :] for k in range(4)])
        turned = keys * cos_rows + pltpu.roll(keys, HD // 2, 1) * sin_rows
        fresh[j, :, 0:HD] = turned.astype(jnp.bfloat16)
        fresh[j, :, HD : 2 * HD] = (term[:, HD : 2 * HD] * factor).astype(jnp.bfloat16)
    for d in order:
        rows = choose(picks[d], [fresh[0], fresh[1]])
        if d == 0:
            kv_fresh[0] = rows
        else:
            stage_fresh[d - 1] = rows
            f_copies[d] = remote(
                stage_fresh.at[d - 1], kv_fresh.at[d], f_send.at[d - 1], f_recv.at[d - 1],
                {"docs": peers[d]},
            )

    for d in (1, 2, 3):
        a_copies[d].wait_recv()
        b_copies[d].wait_recv()
        stored_step(d)

    def fresh_step(near, far):
        page = kv_fresh[near : far + 1].reshape((far + 1 - near) * BLK, 2 * HD)
        source = lax.broadcasted_iota(jnp.int32, (1, page.shape[0]), 1)
        added = jnp.full((1, page.shape[0]), bias[near], jnp.float32)
        for d in range(near + 1, far + 1):
            added = jnp.where(source >= (d - near) * BLK, bias[d], added)
        return page[:, 0:HD], page[:, HD : 2 * HD], added

    f_copies[1].wait_recv()
    f_copies[2].wait_recv()
    f_copies[3].wait_recv()
    half_rows = GQA * half
    heads_tile = tile // half
    o_copy = None
    for turn_of in range(2):
        p = other if turn_of == 0 else s
        query = lax.broadcasted_iota(jnp.int32, (half, HD), 0) + p * half
        for b in range(half_rows // tile):
            at = pl.multiple_of(p * half_rows + b * tile, tile)
            top, row_sum, acc = step(at, *fresh_step(0, 3))
            result = acc * (1.0 / row_sum)
            for k in range(heads_tile):
                piece = jnp.where(query < length, result[k * half : (k + 1) * half, :], 0.0)
                piece = piece.astype(jnp.bfloat16)
                head = b * heads_tile + k
                if turn_of == 0:
                    o_send[:, head * HD : (head + 1) * HD] = piece
                else:
                    out_ref[:, lanes(s * GQA * HD + head * HD, HD)] = piece
        if turn_of == 0:
            o_copy = remote(o_send, out_ref.at[:, lanes(s * GQA * HD, GQA * HD)], o_sems.at[0], o_sems.at[1], partner)

    for copy in chip + s_copies + p_copies:
        copy.wait_send()
    for d in range(1, n_docs):
        a_copies[d].wait_send()
        b_copies[d].wait_send()
        f_copies[d].wait_send()
    o_copy.wait()


def fused(
    hidden_rows, norm_gain, key_weight, value_weight, recompute_block, cache_keys, cache_values,
    slot_of_doc, session_docs, session_count, turn_queries, turn_keys, turn_values, turn_length,
):
    width = hidden_rows.shape[-1]
    half = QLEN // 2
    rows = np.arange(4 * BLK, dtype=np.float64)[:, None]
    angles = rows * ROPE_BASE ** (-np.arange(HD // 2, dtype=np.float64) * 2.0 / HD)[None, :]
    cos_table = np.concatenate([np.cos(angles)] * 2, axis=1).astype(np.float32)
    sin_table = np.concatenate([-np.sin(angles), np.sin(angles)], axis=1).astype(np.float32)
    smem = pl.BlockSpec(memory_space=pltpu.SMEM)
    vmem = pl.BlockSpec(memory_space=pltpu.VMEM)
    hbm = pl.BlockSpec(memory_space=pltpu.HBM)
    bf, f32 = jnp.bfloat16, jnp.float32
    dma = pltpu.SemaphoreType.DMA
    result = pl.pallas_call(
        fused_kernel,
        out_shape=jax.ShapeDtypeStruct((half, 2 * GQA * HD), bf),
        in_specs=[smem] * 5 + [hbm, vmem] + [hbm] * 9,
        out_specs=vmem,
        scratch_shapes=[
            pltpu.VMEM((2, BLK, width), bf),
            pltpu.VMEM((2 * BLK, width), bf),
            pltpu.VMEM((4, width, 2 * HD), bf),
            pltpu.VMEM((2, 2 * BLK, 2 * HD), bf),
            pltpu.VMEM((2, 2 * BLK, 2 * HD), bf),
            pltpu.VMEM((2, half, 2 * HD), bf),
            pltpu.VMEM((3, 3 * BLK, 2 * HD), bf),
            pltpu.VMEM((4, 3 * BLK, 2 * HD), bf),
            pltpu.VMEM((3, BLK, 2 * HD), bf),
            pltpu.VMEM((4, BLK, 2 * HD), bf),
            pltpu.VMEM((2, BLK, 2 * HD), bf),
            pltpu.VMEM((4 * BLK, HD), f32),
            pltpu.VMEM((4 * BLK, HD), f32),
            pltpu.VMEM((3, 2 * BLK, 2 * HD), bf),
            pltpu.VMEM((3, 2 * BLK, 2 * HD), bf),
            pltpu.VMEM((2 * BLK, 2 * HD), f32),
            pltpu.VMEM((8, BLK), f32),
            pltpu.VMEM((3, 8, BLK), f32),
            pltpu.VMEM((QLEN, GQA * HD), bf),
            pltpu.VMEM((QLEN * GQA, HD), bf),
            pltpu.VMEM((QLEN * GQA, 1), f32),
            pltpu.VMEM((QLEN * GQA, 1), f32),
            pltpu.VMEM((QLEN * GQA, HD), f32),
            pltpu.VMEM((half, GQA * HD), bf),
            dma((8,)), dma((8,)), dma((4,)), dma((4,)),
            dma((3,)), dma((3,)), dma((3,)), dma((3,)), dma((3,)), dma((3,)),
            dma((3,)), dma((3,)), dma((3,)), dma((3,)), dma((2,)),
        ],
        compiler_params=pltpu.CompilerParams(
            collective_id=0, has_side_effects=True, vmem_limit_bytes=63 * 1024 * 1024
        ),
        cost_estimate=pl.CostEstimate(
            flops=2_500_000_000, bytes_accessed=8_000_000, transcendentals=3_000_000
        ),
    )(
        session_docs, session_count, slot_of_doc, recompute_block, turn_length,
        hidden_rows, norm_gain, key_weight, value_weight, cache_keys, cache_values,
        jnp.asarray(cos_table), jnp.asarray(sin_table), turn_queries, turn_keys, turn_values,
    )
    return result[None]


def solution(mesh):
    in_specs = (
        P(("parts", "docs"), None, ("heads", "sub")),
        P(("heads", "sub")),
        P(("heads", "sub"), None),
        P(("heads", "sub"), None),
        P(("parts", "docs")),
        P(("parts", "docs"), "sub", "heads"),
        P(("parts", "docs"), "sub", "heads"),
        P("parts"),
        P("parts", None),
        P("parts"),
        P(("parts", "docs"), None, "heads"),
        P(("parts", "docs"), "sub", "heads"),
        P(("parts", "docs"), "sub", "heads"),
        P(("parts", "docs")),
    )
    out_specs = P(("parts", "docs"), "sub", "heads")
    sizes = tuple(mesh.shape[name] for name in ("docs", "heads", "sub"))
    chosen = fused if sizes == (4, 2, 2) else local
    return jax.shard_map(chosen, mesh=mesh, in_specs=in_specs, out_specs=out_specs, check_vma=False)
```

```python
import jax
import jax.numpy as jnp
import numpy as np
from jax import lax
from jax.experimental import pallas as pl
from jax.experimental.pallas import tpu as pltpu
from jax.sharding import PartitionSpec as P

D = 8192
HD = 128
BLK = 128
QLEN = 128
GQA = 8


EPSILON = 1e-05
ROPE_BASE = 500000.0
NEGATIVE = -1e30
LOG2_E = 1.4426950408889634


def rotate(values, positions):
    half_dim = values.shape[-1] // 2
    exponent = jnp.arange(half_dim, dtype=jnp.float32) * (2.0 / values.shape[-1])
    frequency = ROPE_BASE ** (-exponent)
    angles = positions.astype(jnp.float32)[..., None, None] * frequency
    cos_part = jnp.cos(angles)
    sin_part = jnp.sin(angles)
    first_half = values[..., :half_dim]
    second_half = values[..., half_dim:]
    return jnp.concatenate(
        [
            first_half * cos_part - second_half * sin_part,
            second_half * cos_part + first_half * sin_part,
        ],
        axis=-1,
    )


def attend(running, queries, key_rows, value_rows, allowed):
    run_max, run_sum, run_acc = running
    scores = jnp.einsum(
        "qhgd,khd->hgqk", queries, key_rows, preferred_element_type=jnp.float32
    ) * HD ** (-0.5)
    masked = jnp.where(allowed, scores, NEGATIVE)
    new_max = jnp.maximum(run_max, jnp.max(masked, axis=-1))
    weights = jnp.where(allowed, jnp.exp(scores - new_max[..., None]), 0.0)
    factor = jnp.exp(run_max - new_max)
    run_sum = run_sum * factor + jnp.sum(weights, axis=-1)
    update = jnp.einsum(
        "hgqk,khd->hgqd",
        weights.astype(jnp.bfloat16),
        value_rows,
        preferred_element_type=jnp.float32,
    )
    run_acc = run_acc * factor[..., None] + update
    return (new_max, run_sum, run_acc)


def split_page(one_page, kv_local):
    row_count = one_page.shape[0]
    key_rows = one_page[:, : kv_local * HD].reshape(row_count, kv_local, HD)
    value_rows = one_page[:, kv_local * HD :].reshape(row_count, kv_local, HD)
    return (key_rows, value_rows)


def local(
    hidden_rows,
    norm_gain,
    key_weight,
    value_weight,
    recompute_block,
    cache_keys,
    cache_values,
    slot_of_doc,
    session_docs,
    session_count,
    turn_queries,
    turn_keys,
    turn_values,
    turn_length,
):
    heads_here = lax.axis_size("heads")
    parts_sub = lax.axis_size("sub")
    half_index = lax.axis_index("sub")
    session = lax.axis_index("docs")
    docs_here, block_rows, local_width = hidden_rows.shape
    kv_local = cache_keys.shape[-1] // HD
    rows_half = block_rows // parts_sub
    half_rows = cache_keys.shape[1]
    docs_max = session_docs.shape[1]
    squares = jnp.sum(jnp.square(hidden_rows.astype(jnp.float32)), axis=-1)
    squares = lax.psum(squares, ("heads", "sub"))
    row_scale = lax.rsqrt(squares / D + EPSILON)
    scaled = (hidden_rows.astype(jnp.float32) * norm_gain.astype(jnp.float32)).astype(jnp.bfloat16)
    row_pieces = scaled.reshape(docs_here, parts_sub, rows_half, local_width)
    stacked_weights = jnp.stack(
        [
            key_weight.reshape(local_width, heads_here, kv_local * HD),
            value_weight.reshape(local_width, heads_here, kv_local * HD),
        ],
        axis=1,
    )
    partial_terms = jnp.einsum(
        "jsrd,dthc->hsjrtc", row_pieces, stacked_weights, preferred_element_type=jnp.float32
    )
    partial_terms = partial_terms.reshape(
        heads_here * parts_sub * docs_here * rows_half, 2 * kv_local * HD
    )
    own_rows = lax.psum_scatter(
        partial_terms.astype(jnp.bfloat16), ("heads", "sub"), scatter_dimension=0, tiled=True
    ).astype(jnp.float32)
    own_rows = own_rows.reshape(docs_here, rows_half, 2, kv_local, HD)
    own_scale = lax.dynamic_slice_in_dim(row_scale, half_index * rows_half, rows_half, 1)
    own_rows = own_rows * own_scale[:, :, None, None, None]
    row_ids = half_index * rows_half + jnp.arange(rows_half, dtype=jnp.int32)
    positions = recompute_block[:, None] * BLK + row_ids[None, :]
    new_keys = (
        rotate(own_rows[:, :, 0], positions)
        .astype(jnp.bfloat16)
        .reshape(docs_here, rows_half, kv_local * HD)
    )
    new_values = own_rows[:, :, 1].astype(jnp.bfloat16).reshape(docs_here, rows_half, kv_local * HD)
    fresh = jnp.concatenate([new_keys, new_values], axis=-1)
    fresh = lax.all_gather(fresh, "sub", axis=1, tiled=True)
    stored = jnp.concatenate([cache_keys, cache_values], axis=-1)
    global_rows = half_index * half_rows + jnp.arange(half_rows, dtype=jnp.int32)
    offsets = global_rows[None, :] - recompute_block[:, None] * BLK
    inside = (offsets >= 0) & (offsets < BLK)
    picks = jnp.clip(offsets, 0, BLK - 1)
    replaced = jax.vmap(lambda rows_of, row_picks: rows_of[row_picks])(fresh, picks)
    pages = jnp.where(inside[:, :, None], replaced, stored)
    my_docs = lax.dynamic_index_in_dim(session_docs, session, 0, keepdims=False)
    my_count = lax.dynamic_index_in_dim(session_count, session, 0, keepdims=False)
    in_list = jnp.arange(docs_max, dtype=jnp.int32) < my_count
    my_slots = jnp.where(in_list, slot_of_doc[jnp.where(in_list, my_docs, 0)], -1)
    length = turn_length[0]
    queries = turn_queries[0].reshape(QLEN, kv_local, GQA, HD)
    running = (
        jnp.full((kv_local, GQA, QLEN), NEGATIVE, jnp.float32),
        jnp.zeros((kv_local, GQA, QLEN), jnp.float32),
        jnp.zeros((kv_local, GQA, QLEN, HD), jnp.float32),
    )
    turn_rows = turn_keys.shape[1]
    key_ids = half_index * turn_rows + jnp.arange(turn_rows, dtype=jnp.int32)
    query_ids = jnp.arange(QLEN, dtype=jnp.int32)
    turn_seen = (key_ids[None, :] <= query_ids[:, None]) & (key_ids[None, :] < length)
    running = attend(
        running,
        queries,
        turn_keys[0].reshape(turn_rows, kv_local, HD),
        turn_values[0].reshape(turn_rows, kv_local, HD),
        turn_seen[None, None],
    )
    every_row = jnp.ones((1, 1, 1, half_rows), jnp.bool_)
    portion = lax.all_gather(pages, "docs", axis=0, tiled=True)

    def one_slot(position, inner_state):
        one_page = lax.dynamic_index_in_dim(portion, position, 0, keepdims=False)
        key_rows, value_rows = split_page(one_page, kv_local)
        wanted = jnp.any(my_slots == position)
        return lax.cond(
            wanted,
            lambda given: attend(given, queries, key_rows, value_rows, every_row),
            lambda given: given,
            inner_state,
        )

    running = lax.fori_loop(0, portion.shape[0], one_slot, running)
    run_max, run_sum, run_acc = running
    got_max, got_sum, got_acc = (
        lax.all_to_all(
            run_max.astype(jnp.bfloat16), "sub", split_axis=2, concat_axis=2, tiled=True
        ).astype(run_max.dtype),
        lax.all_to_all(
            run_sum.astype(jnp.bfloat16), "sub", split_axis=2, concat_axis=2, tiled=True
        ).astype(run_sum.dtype),
        lax.all_to_all(
            run_acc.astype(jnp.bfloat16), "sub", split_axis=2, concat_axis=2, tiled=True
        ).astype(run_acc.dtype),
    )
    query_half = QLEN // parts_sub
    got_max = got_max.reshape(kv_local, GQA, parts_sub, query_half)
    got_sum = got_sum.reshape(kv_local, GQA, parts_sub, query_half)
    got_acc = got_acc.reshape(kv_local, GQA, parts_sub, query_half, HD)
    joint_max = jnp.max(got_max, axis=2)
    source_weights = jnp.exp(got_max - joint_max[:, :, None, :])
    joint_sum = jnp.sum(got_sum * source_weights, axis=2)
    joint_acc = jnp.sum(got_acc * source_weights[..., None], axis=2)
    result = joint_acc / joint_sum[..., None]
    result = result.transpose(2, 0, 1, 3).reshape(query_half, kv_local * GQA * HD)
    own_queries = half_index * query_half + jnp.arange(query_half, dtype=jnp.int32)
    result = jnp.where(own_queries[:, None] < length, result, 0.0)
    return result.astype(jnp.bfloat16)[None]


def fused_kernel(
    docs_sm, count_sm, slot_sm, block_sm, length_sm,
    hidden_hbm, gain_ref, kw_hbm, vw_hbm, ck_hbm, cv_hbm, cos_hbm, sin_hbm, tq_hbm, tk_hbm, tv_hbm,
    out_ref,
    hid, scaled, wbuf, own, oth, turn, stage, kv, stage_fresh, kv_fresh, fresh, cos_t, sin_t,
    part_out, part_in, part_own, sq_out, sq_in, q_raw, q_all, run_max, run_sum, run_acc, o_send,
    load_sem, w_sem, chip_send, chip_recv, a_send, a_recv, b_send, b_recv, f_send, f_recv,
    p_send, p_recv, s_send, s_recv, o_sems,
):
    z = lax.axis_index("docs")
    h = lax.axis_index("heads")
    s = lax.axis_index("sub")
    n_docs = 4
    other = 1 - s
    mesh_id = pl.DeviceIdType.MESH
    pairs = [(1, 0), (1, 1), (0, 1), (0, 0)]
    peers = [z, z + 1 - 2 * lax.rem(z, 2), lax.rem(z + 2, n_docs), 3 - z]

    def lanes(start, size):
        return pl.ds(pl.multiple_of(start, HD), size)

    my_cols = lanes(s * HD, HD)
    other_cols = lanes(other * HD, HD)

    barrier = pltpu.get_barrier_semaphore()
    for dh, ds in pairs[:3]:
        pl.semaphore_signal(
            barrier, inc=1,
            device_id={"heads": lax.rem(h + dh, 2), "sub": lax.rem(s + ds, 2)},
            device_id_type=mesh_id,
        )
    for d in range(1, n_docs):
        pl.semaphore_signal(
            barrier, inc=1, device_id={"docs": peers[d]}, device_id_type=mesh_id
        )

    loads = [
        (ck_hbm.at[:, :, my_cols], own.at[:, :, 0:HD]),
        (cv_hbm.at[:, :, my_cols], own.at[:, :, HD : 2 * HD]),
        (hidden_hbm, hid),
        (tq_hbm.at[0, :, lanes(s * GQA * HD, GQA * HD)], q_raw),
        (cos_hbm, cos_t),
        (sin_hbm, sin_t),
        (tk_hbm.at[0, :, my_cols], turn.at[s, :, 0:HD]),
        (tv_hbm.at[0, :, my_cols], turn.at[s, :, HD : 2 * HD]),
    ]
    loads = [
        pltpu.make_async_copy(src, dst, load_sem.at[i]) for i, (src, dst) in enumerate(loads)
    ]
    for i in (0, 1, 2):
        loads[i].start()
    w_loads = []
    for i, (dh, ds) in enumerate(pairs):
        head = 2 * lax.rem(h + dh, 2) + lax.rem(s + ds, 2)
        cols = lanes(head * HD, HD)
        w_loads.append(
            [
                pltpu.make_async_copy(kw_hbm.at[:, cols], wbuf.at[i, :, 0:HD], w_sem.at[2 * i]),
                pltpu.make_async_copy(
                    vw_hbm.at[:, cols], wbuf.at[i, :, HD : 2 * HD], w_sem.at[2 * i + 1]
                ),
            ]
        )
        for copy in w_loads[-1]:
            copy.start()
    for i in range(3, len(loads)):
        loads[i].start()

    def remote(src, dst, send, recv, device):
        copy = pltpu.make_async_remote_copy(
            src_ref=src, dst_ref=dst, send_sem=send, recv_sem=recv,
            device_id=device, device_id_type=mesh_id,
        )
        copy.start()
        return copy

    def reads(session, place):
        flag = jnp.int32(0)
        pick = jnp.int32(0)
        for k in range(docs_sm.shape[1]):
            listed = k < count_sm[session]
            doc = docs_sm[session, k]
            slot = jnp.int32(0)
            for j in range(slot_sm.shape[0]):
                slot = jnp.where(doc == j, slot_sm[j], slot)
            local_slot = slot - 2 * place
            hit = listed & (local_slot >= 0) & (local_slot < 2)
            flag = jnp.where(hit, 1, flag)
            pick = jnp.where(hit, local_slot, pick)
        return flag, pick

    picks = [reads(peers[d], z)[1] for d in range(n_docs)]
    bias = []
    for d in range(n_docs):
        flag, _ = reads(z, peers[d])
        bias.append(jnp.where(flag == 1, jnp.float32(0.0), jnp.float32(NEGATIVE)))

    def choose(index, blocks):
        shape = blocks[0].shape
        wide = [block.astype(jnp.float32) for block in blocks]
        chosen = jnp.full(shape, index, jnp.int32)
        result = wide[0]
        for k in range(1, len(wide)):
            result = jnp.where(chosen == k, wide[k], result)
        return result.astype(blocks[0].dtype)

    loads[0].wait()
    loads[1].wait()
    order = (1, 2, 3, 0)
    holds, inner = [], []
    for d in range(n_docs):
        block = jnp.where(picks[d] == 1, block_sm[1], block_sm[0])
        upper = jnp.where(block >= 2, 1, 0)
        holds.append(upper == s)
        inner.append(block - 2 * upper)
    a_copies, b_copies, f_copies = {}, {}, {}
    for d in order:
        at = jnp.where(holds[d], 1 - inner[d], 0)
        rows = choose(picks[d] * 2 + at, [own[j, c * BLK : (c + 1) * BLK, :] for j in range(2) for c in range(2)])
        if d == 0:
            kv[0, 0:BLK, :] = rows
        else:
            stage[d - 1, 0:BLK, :] = rows
    pl.semaphore_wait(barrier, 6)

    partner = {"sub": other}
    chip = [
        remote(ck_hbm.at[:, :, other_cols], oth.at[:, :, 0:HD], chip_send.at[0], chip_recv.at[0], partner),
        remote(cv_hbm.at[:, :, other_cols], oth.at[:, :, HD : 2 * HD], chip_send.at[1], chip_recv.at[1], partner),
        remote(tk_hbm.at[0, :, other_cols], turn.at[s, :, 0:HD], chip_send.at[2], chip_recv.at[2], partner),
        remote(tv_hbm.at[0, :, other_cols], turn.at[s, :, HD : 2 * HD], chip_send.at[3], chip_recv.at[3], partner),
    ]

    for d in (1, 2, 3):
        a_copies[d] = remote(
            stage.at[d - 1, 0:BLK], kv.at[d, 0:BLK], a_send.at[d - 1], a_recv.at[d - 1],
            {"docs": peers[d]},
        )
    chip[0].wait_recv()
    chip[1].wait_recv()
    for d in order:
        at = jnp.where(holds[d], 0, 1 - inner[d])
        second = choose(picks[d] * 2 + at, [oth[j, c * BLK : (c + 1) * BLK, :] for j in range(2) for c in range(2)])
        third = choose(
            picks[d] * 2 + jnp.where(holds[d], 1, 0),
            [half_rows[j, BLK : 2 * BLK, :] for j in range(2) for half_rows in (own, oth)],
        )
        if d == 0:
            kv[0, BLK : 2 * BLK, :] = second
            kv[0, 2 * BLK : 3 * BLK, :] = third
        else:
            stage[d - 1, BLK : 2 * BLK, :] = second
            stage[d - 1, 2 * BLK : 3 * BLK, :] = third
            b_copies[d] = remote(
                stage.at[d - 1, BLK : 3 * BLK], kv.at[d, BLK : 3 * BLK],
                b_send.at[d - 1], b_recv.at[d - 1], {"docs": peers[d]},
            )

    loads[2].wait()
    width = hid.shape[-1]
    gain = gain_ref[...].astype(jnp.float32).reshape(1, width)
    sq_out[...] = jnp.zeros_like(sq_out)
    for j in range(2):
        total = jnp.zeros((BLK, HD), jnp.float32)
        for c in range(width // HD):
            cols = slice(c * HD, (c + 1) * HD)
            x = hid[j, :, cols].astype(jnp.float32)
            total = total + x * x
            scaled[j * BLK : (j + 1) * BLK, cols] = (x * gain[:, cols]).astype(jnp.bfloat16)
        sq_out[j : j + 1, :] = jnp.sum(total.T, axis=0, keepdims=True)
    p_copies, s_copies = [], []
    for i, (dh, ds) in enumerate(pairs):
        for copy in w_loads[i]:
            copy.wait()
        device = {"heads": lax.rem(h + dh, 2), "sub": lax.rem(s + ds, 2)}
        if i < 3:
            s_copies.append(remote(sq_out, sq_in.at[i], s_send.at[i], s_recv.at[i], device))
        term = jnp.dot(scaled[...], wbuf[i], preferred_element_type=jnp.float32)
        if i < 3:
            part_out[i] = term.astype(jnp.bfloat16)
            p_copies.append(
                remote(part_out.at[i], part_in.at[i], p_send.at[i], p_recv.at[i], device)
            )
        else:
            part_own[...] = term

    half = QLEN // 2
    loads[3].wait()
    for p in range(2):
        for head in range(GQA):
            at = (p * GQA + head) * half
            q_all[at : at + half, :] = q_raw[p * half : (p + 1) * half, head * HD : (head + 1) * HD]
    loads[6].wait()
    loads[7].wait()
    chip[2].wait_recv()
    chip[3].wait_recv()
    length = length_sm[0]
    scale = HD ** (-0.5) * LOG2_E
    tile = 256

    def scores_of(at, key_rows):
        return lax.dot_general(
            q_all[pl.ds(at, tile), :], key_rows, (((1,), (1,)), ((), ())),
            preferred_element_type=jnp.float32,
        ) * scale

    def first(b, carry):
        at = pl.multiple_of(b * tile, tile)
        rows = turn[...].reshape(QLEN, 2 * HD)
        scores = scores_of(at, rows[:, 0:HD])
        row = lax.broadcasted_iota(jnp.int32, (tile, QLEN), 0)
        query = (row & (half - 1)) + (b // 2) * half
        key = lax.broadcasted_iota(jnp.int32, (tile, QLEN), 1)
        seen = (key <= query) & (key < length)
        scores = jnp.where(seen, scores, NEGATIVE)
        top = jnp.max(scores, axis=-1, keepdims=True)
        weights = jnp.exp2(scores - top)
        run_max[pl.ds(at, tile), :] = top
        run_sum[pl.ds(at, tile), :] = jnp.sum(weights, axis=-1, keepdims=True)
        run_acc[pl.ds(at, tile), :] = jnp.dot(
            weights.astype(jnp.bfloat16), rows[:, HD : 2 * HD], preferred_element_type=jnp.float32
        )
        return carry

    def step(at, key_rows, value_rows, added):
        scores = scores_of(at, key_rows) + added
        before = run_max[pl.ds(at, tile), :]
        top = jnp.maximum(before, jnp.max(scores, axis=-1, keepdims=True))
        weights = jnp.exp2(scores - top)
        factor = jnp.exp2(before - top)
        row_sum = run_sum[pl.ds(at, tile), :] * factor + jnp.sum(weights, axis=-1, keepdims=True)
        acc = run_acc[pl.ds(at, tile), :] * factor + jnp.dot(
            weights.astype(jnp.bfloat16), value_rows, preferred_element_type=jnp.float32
        )
        return top, row_sum, acc

    def stored_step(d):
        def body(b, carry):
            at = pl.multiple_of(b * tile, tile)
            top, row_sum, acc = step(at, kv[d, :, 0:HD], kv[d, :, HD : 2 * HD], bias[d])
            run_max[pl.ds(at, tile), :] = top
            run_sum[pl.ds(at, tile), :] = row_sum
            run_acc[pl.ds(at, tile), :] = acc
            return carry

        lax.fori_loop(0, q_all.shape[0] // tile, body, 0)

    lax.fori_loop(0, q_all.shape[0] // tile, first, 0)
    stored_step(0)

    loads[4].wait()
    loads[5].wait()
    for copy in s_copies:
        copy.wait_recv()
    for copy in p_copies:
        copy.wait_recv()
    squares = sq_out[...]
    for i in range(3):
        squares = squares + sq_in[i]
    row_scale = lax.rsqrt(squares / D + EPSILON)
    for j in range(2):
        rows = slice(j * BLK, (j + 1) * BLK)
        term = part_own[rows, :]
        for i in range(3):
            term = term + part_in[i, rows, :].astype(jnp.float32)
        factor = jnp.broadcast_to(row_scale[j : j + 1, :], (BLK, HD)).T
        keys = term[:, 0:HD] * factor
        cos_rows = choose(block_sm[j], [cos_t[k * BLK : (k + 1) * BLK, :] for k in range(4)])
        sin_rows = choose(block_sm[j], [sin_t[k * BLK : (k + 1) * BLK, :] for k in range(4)])
        turned = keys * cos_rows + pltpu.roll(keys, HD // 2, 1) * sin_rows
        fresh[j, :, 0:HD] = turned.astype(jnp.bfloat16)
        fresh[j, :, HD : 2 * HD] = (term[:, HD : 2 * HD] * factor).astype(jnp.bfloat16)
    for d in order:
        rows = choose(picks[d], [fresh[0], fresh[1]])
        if d == 0:
            kv_fresh[0] = rows
        else:
            stage_fresh[d - 1] = rows
            f_copies[d] = remote(
                stage_fresh.at[d - 1], kv_fresh.at[d], f_send.at[d - 1], f_recv.at[d - 1],
                {"docs": peers[d]},
            )

    for d in (1, 2, 3):
        a_copies[d].wait_recv()
        b_copies[d].wait_recv()
        stored_step(d)

    def fresh_step(near, far):
        page = kv_fresh[near : far + 1].reshape((far + 1 - near) * BLK, 2 * HD)
        source = lax.broadcasted_iota(jnp.int32, (1, page.shape[0]), 1)
        added = jnp.full((1, page.shape[0]), bias[near], jnp.float32)
        for d in range(near + 1, far + 1):
            added = jnp.where(source >= (d - near) * BLK, bias[d], added)
        return page[:, 0:HD], page[:, HD : 2 * HD], added

    f_copies[1].wait_recv()
    f_copies[2].wait_recv()
    f_copies[3].wait_recv()
    half_rows = GQA * half
    heads_tile = tile // half
    o_copy = None
    for turn_of in range(2):
        p = other if turn_of == 0 else s
        query = lax.broadcasted_iota(jnp.int32, (half, HD), 0) + p * half
        for b in range(half_rows // tile):
            at = pl.multiple_of(p * half_rows + b * tile, tile)
            top, row_sum, acc = step(at, *fresh_step(0, 3))
            result = acc * (1.0 / row_sum)
            for k in range(heads_tile):
                piece = jnp.where(query < length, result[k * half : (k + 1) * half, :], 0.0)
                piece = piece.astype(jnp.bfloat16)
                head = b * heads_tile + k
                if turn_of == 0:
                    o_send[:, head * HD : (head + 1) * HD] = piece
                else:
                    out_ref[:, lanes(s * GQA * HD + head * HD, HD)] = piece
        if turn_of == 0:
            o_copy = remote(o_send, out_ref.at[:, lanes(s * GQA * HD, GQA * HD)], o_sems.at[0], o_sems.at[1], partner)

    for copy in chip + s_copies + p_copies:
        copy.wait_send()
    for d in range(1, n_docs):
        a_copies[d].wait_send()
        b_copies[d].wait_send()
        f_copies[d].wait_send()
    o_copy.wait()


def fused(
    hidden_rows, norm_gain, key_weight, value_weight, recompute_block, cache_keys, cache_values,
    slot_of_doc, session_docs, session_count, turn_queries, turn_keys, turn_values, turn_length,
):
    width = hidden_rows.shape[-1]
    half = QLEN // 2
    rows = np.arange(4 * BLK, dtype=np.float64)[:, None]
    angles = rows * ROPE_BASE ** (-np.arange(HD // 2, dtype=np.float64) * 2.0 / HD)[None, :]
    cos_table = np.concatenate([np.cos(angles)] * 2, axis=1).astype(np.float32)
    sin_table = np.concatenate([-np.sin(angles), np.sin(angles)], axis=1).astype(np.float32)
    smem = pl.BlockSpec(memory_space=pltpu.SMEM)
    vmem = pl.BlockSpec(memory_space=pltpu.VMEM)
    hbm = pl.BlockSpec(memory_space=pltpu.HBM)
    bf, f32 = jnp.bfloat16, jnp.float32
    dma = pltpu.SemaphoreType.DMA
    result = pl.pallas_call(
        fused_kernel,
        out_shape=jax.ShapeDtypeStruct((half, 2 * GQA * HD), bf),
        in_specs=[smem] * 5 + [hbm, vmem] + [hbm] * 9,
        out_specs=vmem,
        scratch_shapes=[
            pltpu.VMEM((2, BLK, width), bf),
            pltpu.VMEM((2 * BLK, width), bf),
            pltpu.VMEM((4, width, 2 * HD), bf),
            pltpu.VMEM((2, 2 * BLK, 2 * HD), bf),
            pltpu.VMEM((2, 2 * BLK, 2 * HD), bf),
            pltpu.VMEM((2, half, 2 * HD), bf),
            pltpu.VMEM((3, 3 * BLK, 2 * HD), bf),
            pltpu.VMEM((4, 3 * BLK, 2 * HD), bf),
            pltpu.VMEM((3, BLK, 2 * HD), bf),
            pltpu.VMEM((4, BLK, 2 * HD), bf),
            pltpu.VMEM((2, BLK, 2 * HD), bf),
            pltpu.VMEM((4 * BLK, HD), f32),
            pltpu.VMEM((4 * BLK, HD), f32),
            pltpu.VMEM((3, 2 * BLK, 2 * HD), bf),
            pltpu.VMEM((3, 2 * BLK, 2 * HD), bf),
            pltpu.VMEM((2 * BLK, 2 * HD), f32),
            pltpu.VMEM((8, BLK), f32),
            pltpu.VMEM((3, 8, BLK), f32),
            pltpu.VMEM((QLEN, GQA * HD), bf),
            pltpu.VMEM((QLEN * GQA, HD), bf),
            pltpu.VMEM((QLEN * GQA, 1), f32),
            pltpu.VMEM((QLEN * GQA, 1), f32),
            pltpu.VMEM((QLEN * GQA, HD), f32),
            pltpu.VMEM((half, GQA * HD), bf),
            dma((8,)), dma((8,)), dma((4,)), dma((4,)),
            dma((3,)), dma((3,)), dma((3,)), dma((3,)), dma((3,)), dma((3,)),
            dma((3,)), dma((3,)), dma((3,)), dma((3,)), dma((2,)),
        ],
        compiler_params=pltpu.CompilerParams(
            collective_id=0, has_side_effects=True, vmem_limit_bytes=63 * 1024 * 1024
        ),
        cost_estimate=pl.CostEstimate(
            flops=2_500_000_000, bytes_accessed=8_000_000, transcendentals=3_000_000
        ),
    )(
        session_docs, session_count, slot_of_doc, recompute_block, turn_length,
        hidden_rows, norm_gain, key_weight, value_weight, cache_keys, cache_values,
        jnp.asarray(cos_table), jnp.asarray(sin_table), turn_queries, turn_keys, turn_values,
    )
    return result[None]


def solution(mesh):
    in_specs = (
        P(("parts", "docs"), None, ("heads", "sub")),
        P(("heads", "sub")),
        P(("heads", "sub"), None),
        P(("heads", "sub"), None),
        P(("parts", "docs")),
        P(("parts", "docs"), "sub", "heads"),
        P(("parts", "docs"), "sub", "heads"),
        P("parts"),
        P("parts", None),
        P("parts"),
        P(("parts", "docs"), None, "heads"),
        P(("parts", "docs"), "sub", "heads"),
        P(("parts", "docs"), "sub", "heads"),
        P(("parts", "docs")),
    )
    out_specs = P(("parts", "docs"), "sub", "heads")
    sizes = tuple(mesh.shape[name] for name in ("docs", "heads", "sub"))
    chosen = fused if sizes == (4, 2, 2) else local
    return jax.shard_map(chosen, mesh=mesh, in_specs=in_specs, out_specs=out_specs, check_vma=False)
```
